512 devices in a mesh: rows: 16 (over z, core), protos: 32 (over x, y).
Axes of the slice: x: 4, y: 8, z: 8, core: 2. Of those that a mesh axis runs over, the one named last changes fastest.
Arguments:
- student_patches: bfloat16 [128, 256, 256], P('rows'), may hold values from -120 to 120
- teacher_patches: bfloat16 [128, 256, 256], P('rows'), may hold values from -120 to 120
- mask_index: int32 [128, 128], P('rows'), may hold values from 0 to 255, as said below
- student_weight: bfloat16 [256, 65536], P(None, 'protos'), may hold values from -140 to 140
- teacher_weight: bfloat16 [256, 65536], P(None, 'protos'), may hold values from -140 to 140
Outputs:
- grad_patches: float32 [128, 256, 256], P('rows', 'protos')
- grad_weight: float32 [256, 65536], P('rows', 'protos')
The draws below stay inside these ranges and needn't reach their ends.
Inputs may be any that keep to these rules, and one draw needn't show every extreme that they name: `mask_index`: each image's 128 entries are distinct patch positions in increasing order.
All inputs are finite; a program needn't handle non-finite values.
Results may differ from the reference program's by a relative error of at most 0.0029.
Values sent between devices are 32-bit elements; how exact they have to be, the bound alone decides.
No kernel may reach another device: no remote copies, remote signals or barrier semaphores. Data moves between devices by JAX's collectives and lax.ppermute only.
A program may use at most 128 MiB of HBM per device.

```python
import math
import jax
import jax.numpy as jnp
from jax import lax

BN = 256
PROTOS = 65536
PATCHES = 256
MASKED = 128
SK_ITERS = 3
IMAGES = 128


def shared_direction(key):
    return jnp.clip(jax.random.normal(jax.random.fold_in(key, 101), (BN,), jnp.float32), -4.0, 4.0)


def weight_base(key):
    return jnp.clip(jax.random.normal(jax.random.fold_in(key, 202), (BN, PROTOS), jnp.float32), -6.0, 6.0)


def draw_student_patches(key, part):
    direction = shared_direction(key)
    key = jax.random.fold_in(key, 11)
    jitter = jnp.clip(jax.random.normal(key, (IMAGES, PATCHES, BN), jnp.float32), -6.0, 6.0)
    rising = 1.5 * jnp.arange(IMAGES, dtype=jnp.float32).reshape(IMAGES, 1, 1) / IMAGES
    return (jitter + rising * direction).astype(jnp.bfloat16)


def draw_teacher_patches(key, part):
    direction = shared_direction(key)
    key = jax.random.fold_in(key, 21)
    jitter = jnp.clip(jax.random.normal(key, (IMAGES, PATCHES, BN), jnp.float32), -6.0, 6.0)
    rising = 1.5 * jnp.arange(IMAGES, dtype=jnp.float32).reshape(IMAGES, 1, 1) / IMAGES
    return (jitter + rising * direction).astype(jnp.bfloat16)


def draw_mask_index(key, part):
    key = jax.random.fold_in(key, 5)
    random_bits = jax.random.randint(key, (IMAGES, PATCHES), 0, 2 ** 20, dtype=jnp.int32)
    scores = random_bits * PATCHES + jnp.arange(PATCHES, dtype=jnp.int32)[None, :]
    ranking = jnp.argsort(scores, axis=1, stable=True)[:, :MASKED]
    return jnp.sort(ranking, axis=1).astype(jnp.int32)


def draw_student_weight(key, part):
    direction = shared_direction(key)
    base_weight = weight_base(key)
    rising = 1.5 * jnp.arange(PROTOS, dtype=jnp.float32).reshape(1, PROTOS) / PROTOS
    return (base_weight + rising * direction[:, None]).astype(jnp.bfloat16)


def draw_teacher_weight(key, part):
    direction = shared_direction(key)
    base_weight = weight_base(key)
    key = jax.random.fold_in(key, 41)
    jitter = 0.3 * jnp.clip(jax.random.normal(jax.random.fold_in(key, 2), (BN, PROTOS), jnp.float32), -6.0, 6.0)
    rising = 1.5 * jnp.arange(PROTOS, dtype=jnp.float32).reshape(1, PROTOS) / PROTOS
    return (base_weight + jitter + rising * direction[:, None]).astype(jnp.bfloat16)


def setup_inputs(seed: int = 0) -> dict:
    streams_of = jax.random.split(jax.random.key(seed), 6)
    student_patches = draw_student_patches(jax.random.fold_in(streams_of[5], 71), 0)
    teacher_patches = draw_teacher_patches(jax.random.fold_in(streams_of[5], 71), 0)
    mask_index = draw_mask_index(jax.random.fold_in(streams_of[5], 71), 0)
    student_weight = draw_student_weight(jax.random.fold_in(streams_of[5], 71), 0)
    teacher_weight = draw_teacher_weight(jax.random.fold_in(streams_of[5], 71), 0)
    return dict(student_patches=student_patches, teacher_patches=teacher_patches, mask_index=mask_index, student_weight=student_weight, teacher_weight=teacher_weight)


epsilon = 1e-06
temp_student = 0.1
temp_teacher = 0.07

def unit_rows(values):
    values = values.astype(jnp.float32)
    length = jnp.sqrt(lax.optimization_barrier(jnp.sum(values * values, axis=-1, keepdims=True)) + epsilon)
    return (values / length, length)

def unit_columns(values):
    values = values.astype(jnp.float32)
    length = jnp.sqrt(lax.optimization_barrier(jnp.sum(values * values, axis=0, keepdims=True)) + epsilon)
    return (values / length, length)

def reference(student_patches, teacher_patches, mask_index, student_weight, teacher_weight):
    images = student_patches.shape[0]
    selector = mask_index[:, :, None]
    picked_student = jnp.take_along_axis(student_patches, selector, axis=1).reshape(-1, BN)
    picked_teacher = jnp.take_along_axis(teacher_patches, selector, axis=1).reshape(-1, BN)
    unit_student, norm_student = unit_rows(picked_student)
    student_unit = unit_student.astype(jnp.bfloat16)
    teacher_unit = unit_rows(picked_teacher)[0].astype(jnp.bfloat16)
    unit_weight, weight_norm = unit_columns(student_weight)
    weight_bf = unit_weight.astype(jnp.bfloat16)
    teacher_bf = unit_columns(teacher_weight)[0].astype(jnp.bfloat16)
    total_rows = picked_student.shape[0]
    block_rows = math.gcd(total_rows, 512)
    block_count = total_rows // block_rows
    teacher_blocks = teacher_unit.reshape(block_count, block_rows, BN)
    student_blocks = student_unit.reshape(block_count, block_rows, BN)

    def teacher_exp(row_block):
        return jnp.exp(jnp.dot(row_block, teacher_bf, preferred_element_type=jnp.float32) * (1.0 / temp_teacher))

    def first_pass(column_total, row_block):
        return (column_total + lax.optimization_barrier(jnp.sum(teacher_exp(row_block), axis=0)), None)
    column_total, _ = lax.scan(first_pass, jnp.zeros((PROTOS,), jnp.float32), teacher_blocks)
    row_scale = jnp.ones((total_rows,), jnp.float32)
    col_scale = jnp.ones((PROTOS,), jnp.float32)
    column_sums = col_scale * column_total
    for sweep in range(SK_ITERS):
        col_scale = col_scale / (column_sums * PROTOS)

        def sweep_rows(column_total, inputs):
            row_block, scaling = inputs
            exp_block = teacher_exp(row_block)
            row_sums = scaling * jnp.dot(exp_block, col_scale, precision=lax.Precision.HIGHEST)
            updated = scaling / (row_sums * total_rows)
            return (column_total + jnp.dot(updated, exp_block, precision=lax.Precision.HIGHEST), updated)
        column_total, updated = lax.scan(sweep_rows, jnp.zeros((PROTOS,), jnp.float32), (teacher_blocks, row_scale.reshape(block_count, block_rows)))
        row_scale = updated.reshape(total_rows)
        column_sums = col_scale * column_total

    def final_pass(weight_total, inputs):
        student_block, teacher_block, scaling = inputs
        logits = jnp.dot(student_block, weight_bf, preferred_element_type=jnp.float32) * (1.0 / temp_student)
        student_exps = jnp.exp(logits)
        probabilities = student_exps / lax.optimization_barrier(jnp.sum(student_exps, axis=1, keepdims=True))
        target = teacher_exp(teacher_block) * scaling[:, None] * (col_scale * total_rows)[None, :]
        score_grad = ((probabilities - target) * (1.0 / temp_student)).astype(jnp.bfloat16)
        feature_part = lax.dot_general(score_grad, weight_bf, (((1,), (1,)), ((), ())), preferred_element_type=jnp.float32)
        weight_part = lax.dot_general(student_block, score_grad, (((0,), (0,)), ((), ())), preferred_element_type=jnp.float32)
        return (weight_total + weight_part, feature_part)
    weight_sum, feature_blocks = lax.scan(final_pass, jnp.zeros((BN, PROTOS), jnp.float32), (student_blocks, teacher_blocks, row_scale.reshape(block_count, block_rows)))
    feature_sum = feature_blocks.reshape(total_rows, BN)
    projection = lax.optimization_barrier(jnp.sum(unit_student * feature_sum, axis=1, keepdims=True))
    masked_grad = ((feature_sum - unit_student * projection) / norm_student).reshape(images, MASKED, BN)
    image_index = lax.broadcasted_iota(jnp.int32, (images, MASKED), 0)
    grad_patches = jnp.zeros((images, PATCHES, BN), jnp.float32).at[image_index, mask_index].set(masked_grad)
    column_dots = lax.optimization_barrier(jnp.sum(unit_weight * weight_sum, axis=0, keepdims=True))
    grad_weight = (weight_sum - unit_weight * column_dots) / weight_norm
    return (grad_patches, grad_weight)
```

```python
import functools
import math

import jax
import jax.numpy as jnp
from jax import lax
from jax.experimental import pallas as pl
from jax.experimental.pallas import tpu as pltpu
from jax.sharding import PartitionSpec as P

PROTOS = 65536
SK_ITERS = 3
LANES = 128

epsilon = 1e-06
temp_student = 0.1
temp_teacher = 0.07

f32 = jnp.float32
bf16 = jnp.bfloat16


def call(body, outs, ins, scratch=(), limit=8, flops=0, moved=0):
    return pl.pallas_call(
        body,
        out_shape=[pltpu.VMEM(s, d) for s, d in outs],
        in_specs=[pl.BlockSpec(memory_space=pltpu.VMEM)] * len(ins),
        out_specs=[pl.BlockSpec(memory_space=pltpu.VMEM)] * len(outs),
        scratch_shapes=list(scratch),
        compiler_params=pltpu.CompilerParams(vmem_limit_bytes=limit * 2**20),
        cost_estimate=pl.CostEstimate(flops=flops, bytes_accessed=moved, transcendentals=0),
    )(*ins)


def selector(mask_ref, image, patches):
    wanted = mask_ref[pl.ds(image, 1), :]
    masked = wanted.shape[1]
    return lax.broadcasted_iota(jnp.int32, (patches, masked), 0) == wanted


def pick(patches_ref, mask_ref, image):
    patches = patches_ref.shape[1]
    chosen = selector(mask_ref, image, patches).astype(bf16)
    return lax.dot_general(
        chosen, patches_ref[image], (((0,), (0,)), ((), ())), preferred_element_type=f32
    )


def lanes_of_rows(parts):
    return jnp.sum(parts.T, axis=0, keepdims=True)


def fold_lanes(values):
    total = values[:, :LANES]
    for start in range(LANES, values.shape[1], LANES):
        total = total + values[:, start : start + LANES]
    return total


def rows_on_sublanes(line):
    pieces = [
        jnp.broadcast_to(line[:, s : s + LANES], (LANES, LANES)).T
        for s in range(0, line.shape[1], LANES)
    ]
    return jnp.concatenate(pieces, axis=0)


def spread(column, width):
    return jnp.concatenate([column] * (width // LANES), axis=1)


def unit_columns(weight_ref, cols):
    weight = weight_ref[:, cols].astype(f32)
    length = jnp.sqrt(jnp.sum(weight * weight, axis=0, keepdims=True) + epsilon)
    return weight / length, length


TILE = 256


def teacher_body(patches_ref, mask_ref, weight_ref, exp_ref, cols_ref, unit_ref):
    images, masked = mask_ref.shape

    def one_image(image, _):
        picked = pick(patches_ref, mask_ref, image)
        length = jnp.sqrt(jnp.sum(picked * picked, axis=1, keepdims=True) + epsilon)
        unit_ref[pl.ds(image * masked, masked), :] = (picked / length).astype(bf16)
        return 0

    lax.fori_loop(0, images, one_image, 0)

    def one_tile(tile, _):
        cols = pl.ds(pl.multiple_of(tile * TILE, TILE), TILE)
        unit = unit_columns(weight_ref, cols)[0].astype(bf16)
        products = jnp.dot(unit_ref[...], unit, preferred_element_type=f32)
        exps = jnp.exp(products * (1.0 / temp_teacher))
        exp_ref[:, cols] = exps
        line = jnp.sum(exps, axis=0, keepdims=True)
        cols_ref[:, :, cols] = jnp.broadcast_to(line[None], (cols_ref.shape[0], 1, TILE))
        return 0

    lax.fori_loop(0, weight_ref.shape[1] // TILE, one_tile, 0)


def student_body(
    patches_ref, mask_ref, weight_ref,
    exp_ref, rows_ref, unit_ref, inverse_ref, turned_ref, back_ref, length_ref, unit_bf_ref, parts_ref,
):
    images, masked = mask_ref.shape

    def one_image(image, _):
        picked = pick(patches_ref, mask_ref, image)
        length = jnp.sqrt(jnp.sum(picked * picked, axis=1, keepdims=True) + epsilon)
        unit = picked / length
        rows = pl.ds(pl.multiple_of(image * masked, masked), masked)
        unit_ref[rows, :] = unit
        unit_bf_ref[rows, :] = unit.astype(bf16)
        turned_ref[:, rows] = unit.T.astype(bf16)
        inverse_ref[rows, :] = jnp.broadcast_to(1.0 / length, (masked, LANES))
        return 0

    lax.fori_loop(0, images, one_image, 0)
    parts_ref[...] = jnp.zeros_like(parts_ref)

    def one_tile(tile, _):
        cols = pl.ds(pl.multiple_of(tile * TILE, TILE), TILE)
        unit, length = unit_columns(weight_ref, cols)
        length_ref[:, cols] = length
        back_ref[cols, :] = unit.T.astype(bf16)
        products = jnp.dot(unit_bf_ref[...], unit.astype(bf16), preferred_element_type=f32)
        exps = jnp.exp(products * (1.0 / temp_student))
        exp_ref[:, cols] = exps
        parts_ref[...] += fold_lanes(exps)
        return 0

    lax.fori_loop(0, weight_ref.shape[1] // TILE, one_tile, 0)
    store_copies(rows_ref, lanes_of_rows(parts_ref[...]))


def store_copies(out_ref, line):
    out_ref[...] = jnp.broadcast_to(line[None], out_ref.shape)


def sum_parts(refs):
    total = None
    for ref in refs:
        line = jnp.sum(ref[...], axis=0)
        total = line if total is None else total + line
    return total


def columns_body(*refs):
    *sums, exp_ref, scale_ref, rows_ref, parts_ref = refs
    scale = 1.0 / (sum_parts(sums) * PROTOS)
    scale_ref[...] = scale
    step = 64

    def block(index, _):
        rows = pl.ds(pl.multiple_of(index * step, step), step)
        total = exp_ref[rows, :LANES] * scale[:, :LANES]
        for start in range(LANES, exp_ref.shape[1], LANES):
            total = total + exp_ref[rows, start : start + LANES] * scale[:, start : start + LANES]
        parts_ref[rows, :] = total
        return 0

    lax.fori_loop(0, exp_ref.shape[0] // step, block, 0)
    store_copies(rows_ref, lanes_of_rows(parts_ref[...]))


def rows_body(total_rows, *refs):
    *sums, exp_ref, cols_ref, scale_ref, parts_ref = refs
    line = 1.0 / (sum_parts(sums)[:, : exp_ref.shape[0]] * total_rows)
    scale_ref[...] = rows_on_sublanes(line)
    width = exp_ref.shape[1]
    parts_ref[...] = jnp.zeros_like(parts_ref)
    step = 64

    def block(index, _):
        rows = pl.ds(pl.multiple_of(index * step, step), step)
        scale = scale_ref[rows, :]
        for start in range(0, width, LANES):
            product = exp_ref[rows, start : start + LANES] * scale
            total = product[0:8]
            for r in range(8, step, 8):
                total = total + product[r : r + 8]
            parts_ref[:, start : start + LANES] += total
        return 0

    lax.fori_loop(0, exp_ref.shape[0] // step, block, 0)
    store_copies(cols_ref, jnp.sum(parts_ref[...], axis=0, keepdims=True))


def placing(mask_ref, image, order, share, patches):
    place = lax.broadcasted_iota(jnp.int32, (patches, mask_ref.shape[1]), 0)
    patch = order(place // share) * share + place % share
    return (patch == mask_ref[pl.ds(image, 1), :]).astype(bf16)


def three_pieces(values):
    high = values.astype(bf16)
    rest = values - high.astype(f32)
    middle = rest.astype(bf16)
    return high, middle, (rest - middle.astype(f32)).astype(bf16)


def feature_body(total_rows, grid, *refs):
    (
        *sums, student_ref, cols_ref, teacher_exp_ref, student_exp_ref, back_ref, unit_ref, inverse_ref, mask_ref,
        first_ref, second_ref, score_ref, row_ref, total_ref, sum_ref,
    ) = refs
    row_ref[...] = rows_on_sublanes(1.0 / (sum_parts(sums) * total_rows))
    total_ref[...] = rows_on_sublanes(1.0 / jnp.sum(student_ref[...], axis=0)[:, teacher_exp_ref.shape[0] :])
    sum_ref[...] = jnp.zeros_like(sum_ref)

    def one_tile(tile, _):
        cols = pl.ds(pl.multiple_of(tile * TILE, TILE), TILE)
        target = teacher_exp_ref[:, cols] * spread(row_ref[...], TILE) * (cols_ref[:, cols] * total_rows)
        probabilities = student_exp_ref[:, cols] * spread(total_ref[...], TILE)
        score = ((probabilities - target) * (1.0 / temp_student)).astype(bf16)
        score_ref[:, cols] = score
        sum_ref[...] += jnp.dot(score, back_ref[cols, :], preferred_element_type=f32)
        return 0

    lax.fori_loop(0, teacher_exp_ref.shape[1] // TILE, one_tile, 0)
    images, masked = mask_ref.shape
    width = unit_ref.shape[1]
    half = width // 2
    size_x, size_y = grid
    shares = size_x * size_y
    patches = first_ref.shape[0] * first_ref.shape[1] // images
    share = patches // shares
    me = lax.axis_index("protos")
    my_x, my_y = me // size_y, me % size_y

    def x_first(place):
        return (place // size_y + my_x) % size_x * size_y + (place % size_y + my_y) % size_y

    def y_first(place):
        return (place % size_x + my_x) % size_x * size_y + (place // size_x + my_y) % size_y

    def one_image(image, _):
        rows = pl.ds(pl.multiple_of(image * masked, masked), masked)
        unit = unit_ref[rows, :]
        total = sum_ref[rows, :]
        projection = jnp.sum(unit * total, axis=1, keepdims=True)
        pieces = three_pieces((total - unit * projection) * spread(inverse_ref[rows, :], width))
        for out_ref, order, lanes in (
            (first_ref, x_first, slice(0, half)),
            (second_ref, y_first, slice(half, width)),
        ):
            chosen = placing(mask_ref, image, order, share, patches)
            placed = sum(jnp.dot(chosen, piece[:, lanes], preferred_element_type=f32) for piece in pieces)
            out_ref[:, pl.ds(pl.multiple_of(image * share, share), share), :] = placed.reshape(
                shares, share, half
            )
        return 0

    lax.fori_loop(0, images, one_image, 0)


def weight_body(shares, score_ref, turned_ref, weight_ref, length_ref, mine_ref, other_ref):
    depth = weight_ref.shape[0]
    share = depth // shares
    levels = shares // 2
    me = lax.axis_index("rows")
    core, level = me % 2, me // 2

    def one_tile(tile, _):
        cols = pl.ds(pl.multiple_of(tile * TILE, TILE), TILE)
        total = jnp.dot(turned_ref[...], score_ref[:, cols], preferred_element_type=f32)
        inverse = 1.0 / length_ref[:, cols]
        unit = weight_ref[:, cols].astype(f32) * inverse
        dots = jnp.sum(unit * total, axis=0, keepdims=True)
        gradient = (total - unit * dots) * inverse
        for z in range(levels):
            even = gradient[2 * z * share : (2 * z + 1) * share]
            odd = gradient[(2 * z + 1) * share : (2 * z + 2) * share]
            place = (z + levels - level) % levels
            mine_ref[pl.ds(place, 1), :, cols] = jnp.where(core == 0, even, odd)[None]
            other_ref[pl.ds(place, 1), :, cols] = jnp.where(core == 0, odd, even)[None]
        return 0

    lax.fori_loop(0, weight_ref.shape[1] // TILE, one_tile, 0)


def add_body(*refs):
    *parts, out_ref = refs
    total = parts[0][...]
    for part in parts[1:]:
        total = total + part[...]
    out_ref[...] = total


def add(*parts):
    (total,) = call(add_body, [(parts[0].shape, f32)], parts, limit=4)
    return total


def moves(axis, size, to):
    return axis, [(i, to(i)) for i in range(size)]


def shift_z(by):
    size = lax.axis_size("rows")
    return moves("rows", size, lambda i: (i + 2 * by) % size)


def swap_rows(bit):
    return moves("rows", lax.axis_size("rows"), lambda i: i ^ bit)


def shift_x(by):
    size = lax.axis_size("protos")
    length = grid_of(size)[1]
    return moves("protos", size, lambda i: (i + length * by) % size)


def shift_y(by):
    size = lax.axis_size("protos")
    length = grid_of(size)[1]
    return moves("protos", size, lambda i: i // length * length + (i + by) % length)


def swap_protos(bit):
    return moves("protos", lax.axis_size("protos"), lambda i: i ^ bit)


def send(values, move):
    axis, pairs = move
    return lax.ppermute(values, axis, pairs)


def grid_of(size):
    return (4, 8) if size == 32 else (2, size // 2)


def by_doubling(line, swaps):
    for move in swaps[:-1]:
        line = add(line, send(line, move))
    return [line, send(line, swaps[-1])]


def all_along(line, shift, size):
    return [line] + [send(line, shift(by)) for by in range(1, size)]


def ring_share(parts, shift, size):
    last = size // 2
    up = parts[last]
    for k in range(last - 1, 0, -1):
        up = send(up, shift(1)) + parts[k]
    up = send(up, shift(1))
    total = parts[0] + up
    if size > 2:
        down = parts[last + 1]
        for k in range(last + 2, size):
            down = send(down, shift(-1)) + parts[k]
        total = total + send(down, shift(-1))
    return total


def everyones(copies, axis):
    return lax.all_to_all(copies, axis, 0, 0, tiled=True)


def local(student_patches, teacher_patches, mask_index, student_weight, teacher_weight):
    images, patches, depth = student_patches.shape
    masked = mask_index.shape[1]
    rows = images * masked
    row_devices = lax.axis_size("rows")
    proto_devices = lax.axis_size("protos")
    total_rows = float(rows * row_devices)
    protos = student_weight.shape[1]
    work = 2 * rows * protos * depth

    teacher_exp, column_part = call(
        teacher_body,
        [((rows, protos), f32), ((row_devices, 1, protos), f32)],
        (teacher_patches, mask_index, teacher_weight),
        [pltpu.VMEM((rows, depth), bf16)],
        flops=work, moved=2**23,
    )
    column_sums = [everyones(column_part, "rows")]
    student_exp, student_part, unit, inverse, turned, back, length = call(
        student_body,
        [
            ((rows, protos), f32),
            ((proto_devices, 1, rows), f32),
            ((rows, depth), f32),
            ((rows, LANES), f32),
            ((depth, rows), bf16),
            ((protos, depth), bf16),
            ((1, protos), f32),
        ],
        (student_patches, mask_index, student_weight),
        [pltpu.VMEM((rows, depth), bf16), pltpu.VMEM((rows, LANES), f32)],
        flops=work, moved=2**23,
    )
    levels = row_devices // 2
    grid = grid_of(proto_devices)
    student_sums = None
    for sweep in range(SK_ITERS):
        col_scale, row_part = call(
            columns_body,
            [((1, protos), f32), ((proto_devices if sweep == 0 else 1, 1, rows), f32)],
            (*column_sums, teacher_exp),
            [pltpu.VMEM((rows, LANES), f32)],
            flops=2 * rows * protos, moved=2**23,
        )
        if sweep == 0:
            student_sums = everyones(jnp.concatenate([row_part, student_part], axis=2), "protos")
            row_sums = [student_sums]
        elif sweep == 1:
            row_sums = all_along(add(*all_along(row_part, shift_x, grid[0])), shift_y, grid[1])
        else:
            row_sums = by_doubling(
                row_part, [swap_protos(1 << bit) for bit in range((proto_devices - 1).bit_length())]
            )
        if sweep < SK_ITERS - 1:
            (column_part,) = call(
                functools.partial(rows_body, total_rows),
                [((1, 1, protos), f32)],
                (*row_sums, teacher_exp),
                [pltpu.VMEM((rows, LANES), f32), pltpu.VMEM((8, protos), f32)],
                flops=2 * rows * protos, moved=2**23,
            )
            if sweep == 0:
                column_sums = all_along(add(column_part, send(column_part, swap_rows(1))), shift_z, levels)
            else:
                column_sums = by_doubling(
                    column_part, [swap_rows(1 << bit) for bit in range((row_devices - 1).bit_length())]
                )
    share = patches // proto_devices
    half = depth // 2
    first, second, score = call(
        functools.partial(feature_body, total_rows, grid),
        [((proto_devices, images * share, half), f32)] * 2 + [((rows, protos), bf16)],
        (*row_sums, student_sums, col_scale, teacher_exp, student_exp, back, unit, inverse, mask_index),
        [
            pltpu.VMEM((rows, LANES), f32),
            pltpu.VMEM((rows, LANES), f32),
            pltpu.VMEM((rows, depth), f32),
        ],
        flops=work, moved=2**24,
    )
    first = first.reshape(grid[0], grid[1], images * share, half)
    second = second.reshape(grid[1], grid[0], images * share, half)
    first = ring_share(ring_share(first, shift_x, grid[0]), shift_y, grid[1])
    second = ring_share(ring_share(second, shift_y, grid[1]), shift_x, grid[0])
    mine, other = call(
        functools.partial(weight_body, row_devices),
        [((levels, depth // row_devices, protos), f32)] * 2,
        (score, turned, student_weight, length),
        flops=work, moved=2**23,
    )
    grad_weight = ring_share(mine + send(other, swap_rows(1)), shift_z, levels)
    grad_patches = jnp.concatenate([first, second], axis=1).reshape(images, share, depth)
    return (grad_patches, grad_weight)


def solution(mesh):
    placed = (
        P("rows", None, None),
        P("rows", None, None),
        P("rows", None),
        P(None, "protos"),
        P(None, "protos"),
    )
    return jax.shard_map(
        local,
        mesh=mesh,
        in_specs=placed,
        out_specs=(P("rows", "protos", None), P("rows", "protos")),
        check_vma=False,
    )
```

```python
import functools
import math

import jax
import jax.numpy as jnp
from jax import lax
from jax.experimental import pallas as pl
from jax.experimental.pallas import tpu as pltpu
from jax.sharding import PartitionSpec as P

PROTOS = 65536
SK_ITERS = 3
LANES = 128

epsilon = 1e-06
temp_student = 0.1
temp_teacher = 0.07

f32 = jnp.float32
bf16 = jnp.bfloat16


def call(body, outs, ins, scratch=(), limit=8, hbm=0, flops=0, moved=0):
    held = [pltpu.with_memory_space_constraint(array, pltpu.HBM) for array in ins[:hbm]]
    spaces = [pltpu.HBM] * hbm + [pltpu.VMEM] * (len(ins) - hbm)
    return pl.pallas_call(
        body,
        out_shape=[pltpu.VMEM(s, d) for s, d in outs],
        in_specs=[pl.BlockSpec(memory_space=space) for space in spaces],
        out_specs=[pl.BlockSpec(memory_space=pltpu.VMEM)] * len(outs),
        scratch_shapes=list(scratch),
        compiler_params=pltpu.CompilerParams(vmem_limit_bytes=limit * 2**20),
        cost_estimate=pl.CostEstimate(flops=flops, bytes_accessed=moved, transcendentals=0),
    )(*held, *ins[hbm:])


def selector(mask_ref, image, patches):
    wanted = mask_ref[pl.ds(image, 1), :]
    masked = wanted.shape[1]
    return lax.broadcasted_iota(jnp.int32, (patches, masked), 0) == wanted


def pick(patches_ref, mask_ref, image):
    patches = patches_ref.shape[1]
    chosen = selector(mask_ref, image, patches).astype(bf16)
    return lax.dot_general(
        chosen, patches_ref[image], (((0,), (0,)), ((), ())), preferred_element_type=f32
    )


def lanes_of_rows(parts):
    return jnp.sum(parts.T, axis=0, keepdims=True)


def fold_lanes(values):
    total = values[:, :LANES]
    for start in range(LANES, values.shape[1], LANES):
        total = total + values[:, start : start + LANES]
    return total


def rows_on_sublanes(line):
    pieces = [
        jnp.broadcast_to(line[:, s : s + LANES], (LANES, LANES)).T
        for s in range(0, line.shape[1], LANES)
    ]
    return jnp.concatenate(pieces, axis=0)


def spread(column, width):
    return jnp.concatenate([column] * (width // LANES), axis=1)


def unit_columns(weight_ref, cols):
    weight = weight_ref[:, cols].astype(f32)
    length = jnp.sqrt(jnp.sum(weight * weight, axis=0, keepdims=True) + epsilon)
    return weight / length, length


TILE = 256
LOG2_E = math.log2(math.e)


def first_body(
    teacher_hbm, teacher_weight_hbm, student_hbm, student_weight_hbm, mask_ref,
    teacher_exp_ref, cols_ref, student_exp_ref, student_rows_ref, unit_ref, inverse_ref, turned_ref, back_ref,
    length_ref,
    teacher_ref, teacher_weight_ref, student_ref, student_weight_ref, teacher_bf_ref, student_bf_ref, parts_ref, sems,
):
    images, masked = mask_ref.shape
    protos = teacher_exp_ref.shape[1]
    loads = [
        pltpu.make_async_copy(source, target, sems.at[index])
        for index, (source, target) in enumerate(
            (
                (teacher_hbm, teacher_ref),
                (teacher_weight_hbm, teacher_weight_ref),
                (student_hbm, student_ref),
                (student_weight_hbm, student_weight_ref),
            )
        )
    ]
    for load in loads:
        load.start()
    loads[0].wait()

    def teacher_image(image, _):
        picked = pick(teacher_ref, mask_ref, image)
        length = jnp.sqrt(jnp.sum(picked * picked, axis=1, keepdims=True) + epsilon)
        rows = pl.ds(pl.multiple_of(image * masked, masked), masked)
        teacher_bf_ref[rows, :] = (picked / length).astype(bf16)
        return 0

    lax.fori_loop(0, images, teacher_image, 0)
    loads[1].wait()

    def teacher_tile(tile, _):
        cols = pl.ds(pl.multiple_of(tile * TILE, TILE), TILE)
        unit = unit_columns(teacher_weight_ref, cols)[0].astype(bf16)
        products = jnp.dot(teacher_bf_ref[...], unit, preferred_element_type=f32)
        exps = jnp.exp2(products * (LOG2_E / temp_teacher))
        teacher_exp_ref[:, cols] = exps
        line = jnp.sum(exps, axis=0, keepdims=True)
        cols_ref[:, :, cols] = jnp.broadcast_to(line[None], (cols_ref.shape[0], 1, TILE))
        return 0

    lax.fori_loop(0, protos // TILE, teacher_tile, 0)
    loads[2].wait()

    def student_image(image, _):
        picked = pick(student_ref, mask_ref, image)
        length = jnp.sqrt(jnp.sum(picked * picked, axis=1, keepdims=True) + epsilon)
        unit = picked / length
        rows = pl.ds(pl.multiple_of(image * masked, masked), masked)
        unit_ref[rows, :] = unit
        student_bf_ref[rows, :] = unit.astype(bf16)
        turned_ref[:, rows] = unit.T.astype(bf16)
        inverse_ref[rows, :] = jnp.broadcast_to(1.0 / length, (masked, LANES))
        return 0

    lax.fori_loop(0, images, student_image, 0)
    parts_ref[...] = jnp.zeros_like(parts_ref)
    loads[3].wait()

    def student_tile(tile, _):
        cols = pl.ds(pl.multiple_of(tile * TILE, TILE), TILE)
        unit, length = unit_columns(student_weight_ref, cols)
        length_ref[:, cols] = length
        back_ref[cols, :] = unit.T.astype(bf16)
        products = jnp.dot(student_bf_ref[...], unit.astype(bf16), preferred_element_type=f32)
        exps = jnp.exp2(products * (LOG2_E / temp_student))
        student_exp_ref[:, cols] = exps
        parts_ref[...] += fold_lanes(exps)
        return 0

    lax.fori_loop(0, protos // TILE, student_tile, 0)
    student_rows_ref[...] = lanes_of_rows(parts_ref[...])


def store_copies(out_ref, line):
    out_ref[...] = jnp.broadcast_to(line[None], out_ref.shape)


def columns_body(sums_ref, exp_ref, *refs):
    *student, scale_ref, rows_ref, parts_ref = refs
    scale = 1.0 / (jnp.sum(sums_ref[...], axis=0) * PROTOS)
    scale_ref[...] = scale
    step = 64

    def block(index, _):
        rows = pl.ds(pl.multiple_of(index * step, step), step)
        total = exp_ref[rows, :LANES] * scale[:, :LANES]
        for start in range(LANES, exp_ref.shape[1], LANES):
            total = total + exp_ref[rows, start : start + LANES] * scale[:, start : start + LANES]
        parts_ref[rows, :] = total
        return 0

    lax.fori_loop(0, exp_ref.shape[0] // step, block, 0)
    line = lanes_of_rows(parts_ref[...])
    if student:
        line = jnp.concatenate([line, student[0][...]], axis=1)
    store_copies(rows_ref, line)


def rows_body(total_rows, sums_ref, exp_ref, cols_ref, scale_ref, parts_ref):
    line = 1.0 / (jnp.sum(sums_ref[...], axis=0)[:, : exp_ref.shape[0]] * total_rows)
    scale_ref[...] = rows_on_sublanes(line)
    width = exp_ref.shape[1]
    parts_ref[...] = jnp.zeros_like(parts_ref)
    step = 64

    def block(index, _):
        rows = pl.ds(pl.multiple_of(index * step, step), step)
        scale = scale_ref[rows, :]
        for start in range(0, width, LANES):
            product = exp_ref[rows, start : start + LANES] * scale
            total = product[0:8]
            for r in range(8, step, 8):
                total = total + product[r : r + 8]
            parts_ref[:, start : start + LANES] += total
        return 0

    lax.fori_loop(0, exp_ref.shape[0] // step, block, 0)
    store_copies(cols_ref, jnp.sum(parts_ref[...], axis=0, keepdims=True))


def three_pieces(values):
    high = values.astype(bf16)
    rest = values - high.astype(f32)
    middle = rest.astype(bf16)
    return high, middle, (rest - middle.astype(f32)).astype(bf16)


def gradient_body(
    total_rows, shares,
    sums_ref, student_ref, cols_ref, teacher_exp_ref, student_exp_ref, back_ref, turned_ref, unit_ref, inverse_ref,
    mask_ref, weight_ref, length_ref,
    placed_ref, weight_out_ref, row_ref, total_ref, sum_ref,
):
    rows = teacher_exp_ref.shape[0]
    row_ref[...] = rows_on_sublanes(1.0 / (jnp.sum(sums_ref[...], axis=0) * total_rows))
    total_ref[...] = rows_on_sublanes((1.0 / temp_student) / jnp.sum(student_ref[...], axis=0)[:, rows:])
    sum_ref[...] = jnp.zeros_like(sum_ref)

    def one_tile(tile, _):
        cols = pl.ds(pl.multiple_of(tile * TILE, TILE), TILE)
        target = teacher_exp_ref[:, cols] * spread(row_ref[...], TILE)
        target = target * (cols_ref[:, cols] * (total_rows / temp_student))
        score = (student_exp_ref[:, cols] * spread(total_ref[...], TILE) - target).astype(bf16)
        total = jnp.dot(turned_ref[...], score, preferred_element_type=f32)
        inverse = 1.0 / length_ref[:, cols]
        unit = weight_ref[:, cols].astype(f32) * inverse
        dots = jnp.sum(unit * total, axis=0, keepdims=True)
        weight_out_ref[:, cols] = (total - unit * dots) * inverse
        sum_ref[...] += jnp.dot(score, back_ref[cols, :], preferred_element_type=f32)
        return 0

    lax.fori_loop(0, teacher_exp_ref.shape[1] // TILE, one_tile, 0)
    images, masked = mask_ref.shape
    width = unit_ref.shape[1]
    patches = placed_ref.shape[0] * placed_ref.shape[1] // images
    share = patches // shares

    def one_image(image, _):
        rows = pl.ds(pl.multiple_of(image * masked, masked), masked)
        unit = unit_ref[rows, :]
        total = sum_ref[rows, :]
        projection = jnp.sum(unit * total, axis=1, keepdims=True)
        pieces = three_pieces((total - unit * projection) * spread(inverse_ref[rows, :], width))
        chosen = selector(mask_ref, image, patches).astype(bf16)
        placed = sum(jnp.dot(chosen, piece, preferred_element_type=f32) for piece in pieces)
        placed_ref[:, pl.ds(pl.multiple_of(image * share, share), share), :] = placed.reshape(
            shares, share, width
        )
        return 0

    lax.fori_loop(0, images, one_image, 0)


def everyones(copies, axis):
    return lax.all_to_all(copies, axis, 0, 0, tiled=True)


def share_of_sum(parts, axis):
    return jnp.sum(lax.all_to_all(parts, axis, 0, 0, tiled=True), axis=0)


def local(student_patches, teacher_patches, mask_index, student_weight, teacher_weight):
    images, patches, depth = student_patches.shape
    masked = mask_index.shape[1]
    rows = images * masked
    row_devices = lax.axis_size("rows")
    proto_devices = lax.axis_size("protos")
    total_rows = float(rows * row_devices)
    protos = student_weight.shape[1]
    work = 2 * rows * protos * depth

    teacher_exp, column_part, student_exp, student_part, unit, inverse, turned, back, length = call(
        first_body,
        [
            ((rows, protos), f32),
            ((row_devices, 1, protos), f32),
            ((rows, protos), f32),
            ((1, rows), f32),
            ((rows, depth), f32),
            ((rows, LANES), f32),
            ((depth, rows), bf16),
            ((protos, depth), bf16),
            ((1, protos), f32),
        ],
        (teacher_patches, teacher_weight, student_patches, student_weight, mask_index),
        [
            pltpu.VMEM(teacher_patches.shape, bf16),
            pltpu.VMEM(teacher_weight.shape, bf16),
            pltpu.VMEM(student_patches.shape, bf16),
            pltpu.VMEM(student_weight.shape, bf16),
            pltpu.VMEM((rows, depth), bf16),
            pltpu.VMEM((rows, depth), bf16),
            pltpu.VMEM((rows, LANES), f32),
            pltpu.SemaphoreType.DMA((4,)),
        ],
        limit=12, hbm=4, flops=2 * work, moved=2**23,
    )
    for sweep in range(SK_ITERS):
        column_sums = everyones(column_part, "rows")
        student = (student_part,) if sweep == 0 else ()
        col_scale, row_part = call(
            columns_body,
            [((1, protos), f32), ((proto_devices, 1, rows * (1 + len(student))), f32)],
            (column_sums, teacher_exp, *student),
            [pltpu.VMEM((rows, LANES), f32)],
            flops=2 * rows * protos, moved=2**23,
        )
        row_sums = everyones(row_part, "protos")
        if sweep == 0:
            student_sums = row_sums
        if sweep < SK_ITERS - 1:
            (column_part,) = call(
                functools.partial(rows_body, total_rows),
                [((row_devices, 1, protos), f32)],
                (row_sums, teacher_exp),
                [pltpu.VMEM((rows, LANES), f32), pltpu.VMEM((8, protos), f32)],
                flops=2 * rows * protos, moved=2**23,
            )
    share = patches // proto_devices
    placed, columns = call(
        functools.partial(gradient_body, total_rows, proto_devices),
        [((proto_devices, images * share, depth), f32), ((depth, protos), f32)],
        (
            row_sums, student_sums, col_scale, teacher_exp, student_exp, back, turned, unit, inverse, mask_index,
            student_weight, length,
        ),
        [
            pltpu.VMEM((rows, LANES), f32),
            pltpu.VMEM((rows, LANES), f32),
            pltpu.VMEM((rows, depth), f32),
        ],
        flops=2 * work, moved=2**24,
    )
    grad_weight = lax.psum_scatter(columns, "rows", scatter_dimension=0, tiled=True)
    grad_patches = share_of_sum(placed, "protos").reshape(images, share, depth)
    return (grad_patches, grad_weight)


def solution(mesh):
    placed = (
        P("rows", None, None),
        P("rows", None, None),
        P("rows", None),
        P(None, "protos"),
        P(None, "protos"),
    )
    return jax.shard_map(
        local,
        mesh=mesh,
        in_specs=placed,
        out_specs=(P("rows", "protos", None), P("rows", "protos")),
        check_vma=False,
    )
```

```python
import functools
import math

import jax
import jax.numpy as jnp
from jax import lax
from jax.experimental import pallas as pl
from jax.experimental.pallas import tpu as pltpu
from jax.sharding import PartitionSpec as P

PROTOS = 65536
SK_ITERS = 3
LANES = 128

epsilon = 1e-06
temp_student = 0.1
temp_teacher = 0.07

f32 = jnp.float32
bf16 = jnp.bfloat16


def call(body, outs, ins, scratch=(), limit=8, hbm=0, flops=0, moved=0):
    held = [pltpu.with_memory_space_constraint(array, pltpu.HBM) for array in ins[:hbm]]
    spaces = [pltpu.HBM] * hbm + [pltpu.VMEM] * (len(ins) - hbm)
    return pl.pallas_call(
        body,
        out_shape=[pltpu.VMEM(s, d) for s, d in outs],
        in_specs=[pl.BlockSpec(memory_space=space) for space in spaces],
        out_specs=[pl.BlockSpec(memory_space=pltpu.VMEM)] * len(outs),
        scratch_shapes=list(scratch),
        compiler_params=pltpu.CompilerParams(vmem_limit_bytes=limit * 2**20),
        cost_estimate=pl.CostEstimate(flops=flops, bytes_accessed=moved, transcendentals=0),
    )(*held, *ins[hbm:])


def selector(mask_ref, image, patches):
    wanted = mask_ref[pl.ds(image, 1), :]
    masked = wanted.shape[1]
    return lax.broadcasted_iota(jnp.int32, (patches, masked), 0) == wanted


def pick(patches_ref, mask_ref, image):
    patches = patches_ref.shape[1]
    chosen = selector(mask_ref, image, patches).astype(bf16)
    return lax.dot_general(
        chosen, patches_ref[image], (((0,), (0,)), ((), ())), preferred_element_type=f32
    )


def lanes_of_rows(parts):
    return jnp.sum(parts.T, axis=0, keepdims=True)


def fold_lanes(values):
    total = values[:, :LANES]
    for start in range(LANES, values.shape[1], LANES):
        total = total + values[:, start : start + LANES]
    return total


def rows_on_sublanes(line):
    pieces = [
        jnp.broadcast_to(line[:, s : s + LANES], (LANES, LANES)).T
        for s in range(0, line.shape[1], LANES)
    ]
    return jnp.concatenate(pieces, axis=0)


def spread(column, width):
    return jnp.concatenate([column] * (width // LANES), axis=1)


def unit_columns(weight_ref, cols):
    weight = weight_ref[:, cols].astype(f32)
    length = jnp.sqrt(jnp.sum(weight * weight, axis=0, keepdims=True) + epsilon)
    return weight * (1.0 / length), length


TILE = 256
LOG2_E = math.log2(math.e)


def first_body(
    teacher_hbm, teacher_weight_hbm, student_hbm, student_weight_hbm, mask_ref,
    teacher_exp_ref, cols_ref, student_exp_ref, student_rows_ref, unit_ref, inverse_ref, turned_ref, back_ref,
    length_ref,
    teacher_ref, teacher_weight_ref, student_ref, student_weight_ref, teacher_bf_ref, student_bf_ref, parts_ref, sems,
):
    images, masked = mask_ref.shape
    protos = teacher_exp_ref.shape[1]
    loads = [
        pltpu.make_async_copy(source, target, sems.at[index])
        for index, (source, target) in enumerate(
            (
                (teacher_hbm, teacher_ref),
                (teacher_weight_hbm, teacher_weight_ref),
                (student_hbm, student_ref),
                (student_weight_hbm, student_weight_ref),
            )
        )
    ]
    for load in loads:
        load.start()
    loads[0].wait()

    def teacher_image(image, _):
        picked = pick(teacher_ref, mask_ref, image)
        length = jnp.sqrt(jnp.sum(picked * picked, axis=1, keepdims=True) + epsilon)
        rows = pl.ds(pl.multiple_of(image * masked, masked), masked)
        teacher_bf_ref[rows, :] = (picked * (1.0 / length)).astype(bf16)
        return 0

    lax.fori_loop(0, images, teacher_image, 0, unroll=2)
    loads[1].wait()

    def teacher_tile(tile, _):
        cols = pl.ds(pl.multiple_of(tile * TILE, TILE), TILE)
        unit = unit_columns(teacher_weight_ref, cols)[0].astype(bf16)
        products = jnp.dot(teacher_bf_ref[...], unit, preferred_element_type=f32)
        exps = jnp.exp2(products * (LOG2_E / temp_teacher))
        teacher_exp_ref[:, cols] = exps
        line = jnp.sum(exps, axis=0, keepdims=True)
        cols_ref[:, :, cols] = jnp.broadcast_to(line[None], (cols_ref.shape[0], 1, TILE))
        return 0

    lax.fori_loop(0, protos // TILE, teacher_tile, 0, unroll=2)
    loads[2].wait()

    def student_image(image, _):
        picked = pick(student_ref, mask_ref, image)
        length = jnp.sqrt(jnp.sum(picked * picked, axis=1, keepdims=True) + epsilon)
        inverse = 1.0 / length
        unit = picked * inverse
        rows = pl.ds(pl.multiple_of(image * masked, masked), masked)
        unit_ref[rows, :] = unit
        student_bf_ref[rows, :] = unit.astype(bf16)
        turned_ref[:, rows] = unit.T.astype(bf16)
        inverse_ref[rows, :] = jnp.broadcast_to(inverse, (masked, LANES))
        return 0

    lax.fori_loop(0, images, student_image, 0, unroll=2)
    parts_ref[...] = jnp.zeros_like(parts_ref)
    loads[3].wait()

    def student_tile(tile, _):
        cols = pl.ds(pl.multiple_of(tile * TILE, TILE), TILE)
        unit, length = unit_columns(student_weight_ref, cols)
        length_ref[:, cols] = length
        back_ref[cols, :] = unit.T.astype(bf16)
        products = jnp.dot(student_bf_ref[...], unit.astype(bf16), preferred_element_type=f32)
        exps = jnp.exp2(products * (LOG2_E / temp_student))
        student_exp_ref[:, cols] = exps
        parts_ref[...] += fold_lanes(exps)
        return 0

    lax.fori_loop(0, protos // TILE, student_tile, 0, unroll=2)
    student_rows_ref[...] = lanes_of_rows(parts_ref[...])


def store_copies(out_ref, line):
    out_ref[...] = jnp.broadcast_to(line[None], out_ref.shape)


def columns_body(sums_ref, exp_ref, *refs):
    *student, scale_ref, rows_ref, parts_ref = refs
    scale = 1.0 / (jnp.sum(sums_ref[...], axis=0) * PROTOS)
    scale_ref[...] = scale
    step = 64

    def block(index, _):
        rows = pl.ds(pl.multiple_of(index * step, step), step)
        total = exp_ref[rows, :LANES] * scale[:, :LANES]
        for start in range(LANES, exp_ref.shape[1], LANES):
            total = total + exp_ref[rows, start : start + LANES] * scale[:, start : start + LANES]
        parts_ref[rows, :] = total
        return 0

    lax.fori_loop(0, exp_ref.shape[0] // step, block, 0, unroll=2)
    line = lanes_of_rows(parts_ref[...])
    if student:
        line = jnp.concatenate([line, student[0][...]], axis=1)
    store_copies(rows_ref, line)


def rows_body(total_rows, sums_ref, exp_ref, cols_ref, scale_ref, parts_ref):
    line = 1.0 / (jnp.sum(sums_ref[...], axis=0)[:, : exp_ref.shape[0]] * total_rows)
    scale_ref[...] = rows_on_sublanes(line)
    width = exp_ref.shape[1]
    parts_ref[...] = jnp.zeros_like(parts_ref)
    step = 64

    def block(index, _):
        rows = pl.ds(pl.multiple_of(index * step, step), step)
        scale = scale_ref[rows, :]
        for start in range(0, width, LANES):
            product = exp_ref[rows, start : start + LANES] * scale
            total = product[0:8]
            for r in range(8, step, 8):
                total = total + product[r : r + 8]
            parts_ref[:, start : start + LANES] += total
        return 0

    lax.fori_loop(0, exp_ref.shape[0] // step, block, 0, unroll=2)
    store_copies(cols_ref, jnp.sum(parts_ref[...], axis=0, keepdims=True))


def three_pieces(values):
    high = values.astype(bf16)
    rest = values - high.astype(f32)
    middle = rest.astype(bf16)
    return high, middle, (rest - middle.astype(f32)).astype(bf16)


def gradient_body(
    total_rows, shares,
    sums_ref, student_ref, cols_ref, teacher_exp_ref, student_exp_ref, back_ref, turned_ref, unit_ref, inverse_ref,
    mask_ref, weight_ref, length_ref,
    placed_ref, mine_ref, other_ref, row_ref, total_ref, sum_ref, score_ref,
):
    rows = teacher_exp_ref.shape[0]
    row_ref[...] = rows_on_sublanes(1.0 / (jnp.sum(sums_ref[...], axis=0) * total_rows))
    total_ref[...] = rows_on_sublanes((1.0 / temp_student) / jnp.sum(student_ref[...], axis=0)[:, rows:])
    levels, depth_share = mine_ref.shape[:2]
    me = lax.axis_index("rows")
    core, level = me % 2, me // 2

    def one_tile(tile, _):
        cols = pl.ds(pl.multiple_of(tile * TILE, TILE), TILE)
        target = teacher_exp_ref[:, cols] * spread(row_ref[...], TILE)
        target = target * (cols_ref[:, cols] * (total_rows / temp_student))
        score = (student_exp_ref[:, cols] * spread(total_ref[...], TILE) - target).astype(bf16)
        total = jnp.dot(turned_ref[...], score, preferred_element_type=f32)
        inverse = 1.0 / length_ref[:, cols]
        unit = weight_ref[:, cols].astype(f32) * inverse
        dots = jnp.sum(unit * total, axis=0, keepdims=True)
        gradient = ((total - unit * dots) * inverse).reshape(levels, 2, depth_share, TILE)
        for z in range(levels):
            place = pl.ds((z + levels - level) % levels, 1)
            mine_ref[place, :, cols] = jnp.where(core == 0, gradient[z, 0], gradient[z, 1])[None]
            other_ref[place, :, cols] = jnp.where(core == 0, gradient[z, 1], gradient[z, 0])[None]
        score_ref[:, cols] = score
        return 0

    lax.fori_loop(0, teacher_exp_ref.shape[1] // TILE, one_tile, 0, unroll=2)
    sum_ref[...] = jnp.dot(score_ref[...], back_ref[...], preferred_element_type=f32)
    images, masked = mask_ref.shape
    width = unit_ref.shape[1]
    patches = placed_ref.shape[0] * placed_ref.shape[1] // images
    share = patches // shares

    def one_image(image, _):
        rows = pl.ds(pl.multiple_of(image * masked, masked), masked)
        unit = unit_ref[rows, :]
        total = sum_ref[rows, :]
        projection = jnp.sum(unit * total, axis=1, keepdims=True)
        pieces = three_pieces((total - unit * projection) * spread(inverse_ref[rows, :], width))
        chosen = selector(mask_ref, image, patches).astype(bf16)
        placed = sum(jnp.dot(chosen, piece, preferred_element_type=f32) for piece in pieces)
        placed_ref[:, pl.ds(pl.multiple_of(image * share, share), share), :] = placed.reshape(
            shares, share, width
        )
        return 0

    lax.fori_loop(0, images, one_image, 0, unroll=2)


def everyones(copies, axis):
    return lax.all_to_all(copies, axis, 0, 0, tiled=True)


def share_of_sum(parts, axis):
    return jnp.sum(lax.all_to_all(parts, axis, 0, 0, tiled=True), axis=0)


def send_rows(values, to):
    return lax.ppermute(values, "rows", [(i, to(i)) for i in range(lax.axis_size("rows"))])


def local(student_patches, teacher_patches, mask_index, student_weight, teacher_weight):
    images, patches, depth = student_patches.shape
    masked = mask_index.shape[1]
    rows = images * masked
    row_devices = lax.axis_size("rows")
    proto_devices = lax.axis_size("protos")
    total_rows = float(rows * row_devices)
    protos = student_weight.shape[1]
    work = 2 * rows * protos * depth

    teacher_exp, column_part, student_exp, student_part, unit, inverse, turned, back, length = call(
        first_body,
        [
            ((rows, protos), f32),
            ((row_devices, 1, protos), f32),
            ((rows, protos), f32),
            ((1, rows), f32),
            ((rows, depth), f32),
            ((rows, LANES), f32),
            ((depth, rows), bf16),
            ((protos, depth), bf16),
            ((1, protos), f32),
        ],
        (teacher_patches, teacher_weight, student_patches, student_weight, mask_index),
        [
            pltpu.VMEM(teacher_patches.shape, bf16),
            pltpu.VMEM(teacher_weight.shape, bf16),
            pltpu.VMEM(student_patches.shape, bf16),
            pltpu.VMEM(student_weight.shape, bf16),
            pltpu.VMEM((rows, depth), bf16),
            pltpu.VMEM((rows, depth), bf16),
            pltpu.VMEM((rows, LANES), f32),
            pltpu.SemaphoreType.DMA((4,)),
        ],
        limit=12, hbm=4, flops=2 * work, moved=2**23,
    )
    for sweep in range(SK_ITERS):
        column_sums = everyones(column_part, "rows")
        student = (student_part,) if sweep == 0 else ()
        col_scale, row_part = call(
            columns_body,
            [((1, protos), f32), ((proto_devices, 1, rows * (1 + len(student))), f32)],
            (column_sums, teacher_exp, *student),
            [pltpu.VMEM((rows, LANES), f32)],
            flops=2 * rows * protos, moved=2**23,
        )
        row_sums = everyones(row_part, "protos")
        if sweep == 0:
            student_sums = row_sums
        if sweep < SK_ITERS - 1:
            (column_part,) = call(
                functools.partial(rows_body, total_rows),
                [((row_devices, 1, protos), f32)],
                (row_sums, teacher_exp),
                [pltpu.VMEM((rows, LANES), f32), pltpu.VMEM((8, protos), f32)],
                flops=2 * rows * protos, moved=2**23,
            )
    share = patches // proto_devices
    levels = row_devices // 2
    placed, mine, other = call(
        functools.partial(gradient_body, total_rows, proto_devices),
        [((proto_devices, images * share, depth), f32)] + [((levels, depth // row_devices, protos), f32)] * 2,
        (
            row_sums, student_sums, col_scale, teacher_exp, student_exp, back, turned, unit, inverse, mask_index,
            student_weight, length,
        ),
        [
            pltpu.VMEM((rows, LANES), f32),
            pltpu.VMEM((rows, LANES), f32),
            pltpu.VMEM((rows, depth), f32),
            pltpu.VMEM((rows, protos), bf16),
        ],
        limit=12, flops=2 * work, moved=2**24,
    )
    levels_parts = mine + send_rows(other, lambda i: i ^ 1)
    grad_weight = levels_parts[0]
    for ahead in range(1, levels):
        grad_weight = grad_weight + send_rows(levels_parts[ahead], lambda i: (i + 2 * ahead) % row_devices)
    grad_patches = share_of_sum(placed, "protos").reshape(images, share, depth)
    return (grad_patches, grad_weight)


def solution(mesh):
    placed = (
        P("rows", None, None),
        P("rows", None, None),
        P("rows", None),
        P(None, "protos"),
        P(None, "protos"),
    )
    return jax.shard_map(
        local,
        mesh=mesh,
        in_specs=placed,
        out_specs=(P("rows", "protos", None), P("rows", "protos")),
        check_vma=False,
    )
```

```python
import functools
import math

import jax
import jax.numpy as jnp
from jax import lax
from jax.experimental import pallas as pl
from jax.experimental.pallas import tpu as pltpu
from jax.sharding import PartitionSpec as P

PROTOS = 65536
SK_ITERS = 3
LANES = 128

epsilon = 1e-06
temp_student = 0.1
temp_teacher = 0.07

f32 = jnp.float32
bf16 = jnp.bfloat16


def call(body, outs, ins, scratch=(), limit=8, hbm=0, flops=0, moved=0):
    held = [pltpu.with_memory_space_constraint(array, pltpu.HBM) for array in ins[:hbm]]
    spaces = [pltpu.HBM] * hbm + [pltpu.VMEM] * (len(ins) - hbm)
    return pl.pallas_call(
        body,
        out_shape=[pltpu.VMEM(s, d) for s, d in outs],
        in_specs=[pl.BlockSpec(memory_space=space) for space in spaces],
        out_specs=[pl.BlockSpec(memory_space=pltpu.VMEM)] * len(outs),
        scratch_shapes=list(scratch),
        compiler_params=pltpu.CompilerParams(vmem_limit_bytes=limit * 2**20),
        cost_estimate=pl.CostEstimate(flops=flops, bytes_accessed=moved, transcendentals=0),
    )(*held, *ins[hbm:])


def pick(patches_ref, positions, image):
    patches = patches_ref.shape[1]
    masked = positions.shape[0]
    column = lax.broadcasted_iota(jnp.int32, (masked, patches), 1).astype(f32)
    chosen = (column == positions[:, image : image + 1]).astype(bf16)
    return jnp.dot(chosen, patches_ref[image], preferred_element_type=f32)


def lanes_of_rows(parts):
    groups = parts.shape[0] // LANES
    lane = lax.broadcasted_iota(jnp.int32, (LANES, LANES), 1)
    table = jnp.zeros((LANES, LANES), f32)
    for group in range(groups):
        column = jnp.sum(parts[group * LANES : (group + 1) * LANES], axis=1, keepdims=True)
        table = jnp.where(lane == group, column, table)
    table = table.T
    return jnp.concatenate([table[group : group + 1] for group in range(groups)], axis=1)


def fold_lanes(values):
    total = values[:, :LANES]
    for start in range(LANES, values.shape[1], LANES):
        total = total + values[:, start : start + LANES]
    return total


def rows_on_sublanes(line):
    groups = line.shape[1] // LANES
    table = jnp.concatenate([line[:, g * LANES : (g + 1) * LANES] for g in range(groups)], axis=0).T
    pieces = [jnp.broadcast_to(table[:, g : g + 1], (LANES, LANES)) for g in range(groups)]
    return jnp.concatenate(pieces, axis=0)


def spread(column, width):
    return jnp.concatenate([column] * (width // LANES), axis=1)


def unit_columns(weight_ref, cols):
    weight = weight_ref[:, cols].astype(f32)
    length = jnp.sqrt(jnp.sum(weight * weight, axis=0, keepdims=True) + epsilon)
    return weight * (1.0 / length), length


TILE = 256
LOG2_E = math.log2(math.e)


def first_body(
    teacher_hbm, teacher_weight_hbm, student_hbm, student_weight_hbm, mask_hbm,
    teacher_exp_ref, cols_ref, student_exp_ref, student_rows_ref, unit_ref, inverse_ref, turned_ref, unit_weight_ref,
    length_ref,
    teacher_ref, teacher_weight_ref, student_ref, student_weight_ref, mask_ref, teacher_bf_ref, student_bf_ref, parts_ref, sems,
):
    images, masked = mask_ref.shape
    protos = teacher_exp_ref.shape[1]
    loads = [
        pltpu.make_async_copy(source, target, sems.at[index])
        for index, (source, target) in enumerate(
            (
                (mask_hbm, mask_ref),
                (teacher_hbm, teacher_ref),
                (teacher_weight_hbm, teacher_weight_ref),
                (student_hbm, student_ref),
                (student_weight_hbm, student_weight_ref),
            )
        )
    ]
    for load in loads:
        load.start()
    loads[0].wait()
    positions = mask_ref[...].astype(f32).T
    loads[1].wait()
    for image in range(images):
        picked = pick(teacher_ref, positions, image)
        length = jnp.sqrt(jnp.sum(picked * picked, axis=1, keepdims=True) + epsilon)
        rows = slice(image * masked, (image + 1) * masked)
        teacher_bf_ref[rows, :] = (picked * (1.0 / length)).astype(bf16)
    loads[2].wait()

    def teacher_tile(tile, _):
        cols = pl.ds(pl.multiple_of(tile * TILE, TILE), TILE)
        unit = unit_columns(teacher_weight_ref, cols)[0].astype(bf16)
        products = jnp.dot(teacher_bf_ref[...], unit, preferred_element_type=f32)
        exps = jnp.exp2(products * (LOG2_E / temp_teacher))
        teacher_exp_ref[:, cols] = exps
        line = jnp.sum(exps, axis=0, keepdims=True)
        cols_ref[:, :, cols] = jnp.broadcast_to(line[None], (cols_ref.shape[0], 1, TILE))
        return 0

    lax.fori_loop(0, protos // TILE, teacher_tile, 0, unroll=4)
    loads[3].wait()

    for image in range(images):
        picked = pick(student_ref, positions, image)
        inverse = 1.0 / jnp.sqrt(jnp.sum(picked * picked, axis=1, keepdims=True) + epsilon)
        unit = picked * inverse
        rows = slice(image * masked, (image + 1) * masked)
        unit_ref[rows, :] = unit
        student_bf_ref[rows, :] = unit.astype(bf16)
        turned_ref[:, rows] = unit.T.astype(bf16)
        inverse_ref[rows, :] = jnp.broadcast_to(inverse, (masked, LANES))
    parts_ref[...] = jnp.zeros_like(parts_ref)
    loads[4].wait()

    def student_tile(tile, _):
        cols = pl.ds(pl.multiple_of(tile * TILE, TILE), TILE)
        unit, length = unit_columns(student_weight_ref, cols)
        length_ref[:, cols] = length
        unit = unit.astype(bf16)
        unit_weight_ref[:, cols] = unit
        products = jnp.dot(student_bf_ref[...], unit, preferred_element_type=f32)
        exps = jnp.exp2(products * (LOG2_E / temp_student))
        student_exp_ref[:, cols] = exps
        parts_ref[...] += fold_lanes(exps)
        return 0

    lax.fori_loop(0, protos // TILE, student_tile, 0, unroll=4)
    student_rows_ref[...] = lanes_of_rows(parts_ref[...])


def store_copies(out_ref, line):
    out_ref[...] = jnp.broadcast_to(line[None], out_ref.shape)


def columns_body(sums_ref, exp_ref, *refs):
    *rider, scale_ref, rows_ref, parts_ref = refs
    scale = 1.0 / (jnp.sum(sums_ref[...], axis=0) * PROTOS)
    scale_ref[...] = scale
    step = 64

    def block(index, _):
        rows = pl.ds(pl.multiple_of(index * step, step), step)
        total = exp_ref[rows, :LANES] * scale[:, :LANES]
        for start in range(LANES, exp_ref.shape[1], LANES):
            total = total + exp_ref[rows, start : start + LANES] * scale[:, start : start + LANES]
        parts_ref[rows, :] = total
        return 0

    lax.fori_loop(0, exp_ref.shape[0] // step, block, 0, unroll=2)
    line = lanes_of_rows(parts_ref[...])
    peers, _, width = rows_ref.shape
    rows = line.shape[1]
    rows_ref[:, :, :rows] = jnp.broadcast_to(line[None], (peers, 1, rows))
    if rider:
        groups = rider[0].shape[1] // LANES
        for group in range(groups):
            lanes = rider[0][:, group * LANES : (group + 1) * LANES]
            some = slice(group * peers // groups, (group + 1) * peers // groups)
            rows_ref[some, :, rows:] = jnp.broadcast_to(lanes[None], (peers // groups, 1, LANES))


def rows_body(total_rows, sums_ref, exp_ref, cols_ref, *refs):
    *rider, scale_ref, parts_ref = refs
    sums = jnp.sum(sums_ref[...], axis=0)
    line = 1.0 / (sums[:, : exp_ref.shape[0]] * total_rows)
    if rider:
        rider[0][...] = sums[:, exp_ref.shape[0] :]
    scale_ref[...] = rows_on_sublanes(line)
    width = exp_ref.shape[1]
    parts_ref[...] = jnp.zeros_like(parts_ref)
    step = 64

    def block(index, _):
        rows = pl.ds(pl.multiple_of(index * step, step), step)
        scale = scale_ref[rows, :]
        for start in range(0, width, LANES):
            product = exp_ref[rows, start : start + LANES] * scale
            total = product[0:8]
            for r in range(8, step, 8):
                total = total + product[r : r + 8]
            parts_ref[:, start : start + LANES] += total
        return 0

    lax.fori_loop(0, exp_ref.shape[0] // step, block, 0, unroll=2)
    store_copies(cols_ref, jnp.sum(parts_ref[...], axis=0, keepdims=True))


def three_pieces(values):
    high = values.astype(bf16)
    rest = values - high.astype(f32)
    middle = rest.astype(bf16)
    return high, middle, (rest - middle.astype(f32)).astype(bf16)


def gradient_body(
    total_rows,
    sums_ref, student_ref, cols_ref, teacher_exp_ref, student_exp_ref, unit_weight_ref, turned_ref, unit_ref, inverse_ref,
    mask_ref, weight_ref, length_ref,
    placed_ref, mine_ref, other_ref,
    row_ref, total_ref, sum_ref, score_ref,
):
    rows = teacher_exp_ref.shape[0]
    row_ref[...] = rows_on_sublanes(1.0 / (jnp.sum(sums_ref[...], axis=0) * total_rows))
    groups = rows // LANES
    step = student_ref.shape[0] // groups
    totals = jnp.concatenate([student_ref[group * step][:, rows:] for group in range(groups)], axis=1)
    total_ref[...] = rows_on_sublanes((1.0 / temp_student) / totals)
    levels, depth_share = mine_ref.shape[:2]
    me = lax.axis_index("rows")
    core, level = me % 2, me // 2

    def one_tile(tile, _):
        cols = pl.ds(pl.multiple_of(tile * TILE, TILE), TILE)
        target = teacher_exp_ref[:, cols] * spread(row_ref[...], TILE)
        target = target * (cols_ref[:, cols] * (total_rows / temp_student))
        score = (student_exp_ref[:, cols] * spread(total_ref[...], TILE) - target).astype(bf16)
        total = jnp.dot(turned_ref[...], score, preferred_element_type=f32)
        inverse = 1.0 / length_ref[:, cols]
        unit = weight_ref[:, cols].astype(f32) * inverse
        dots = jnp.sum(unit * total, axis=0, keepdims=True)
        gradient = ((total - unit * dots) * inverse).reshape(levels, 2, depth_share, TILE)
        for z in range(levels):
            place = pl.ds((z + levels - level) % levels, 1)
            mine_ref[place, :, cols] = jnp.where(core == 0, gradient[z, 0], gradient[z, 1])[None]
            other_ref[place, :, cols] = jnp.where(core == 0, gradient[z, 1], gradient[z, 0])[None]
        score_ref[:, cols] = score
        return 0

    lax.fori_loop(0, teacher_exp_ref.shape[1] // TILE, one_tile, 0, unroll=2)
    sum_ref[...] = lax.dot_general(
        score_ref[...], unit_weight_ref[...], (((1,), (1,)), ((), ())), preferred_element_type=f32
    )
    images, masked = mask_ref.shape
    width = unit_ref.shape[1]
    shares = placed_ref.shape[0]
    share = placed_ref.shape[1] // images
    patch = lax.broadcasted_iota(jnp.int32, (shares * share, masked), 0)

    def one_image(image, _):
        rows = pl.ds(pl.multiple_of(image * masked, masked), masked)
        unit = unit_ref[rows, :]
        total = sum_ref[rows, :]
        projection = jnp.sum(unit * total, axis=1, keepdims=True)
        pieces = three_pieces((total - unit * projection) * spread(inverse_ref[rows, :], width))
        chosen = (patch == mask_ref[pl.ds(image, 1), :]).astype(bf16)
        placed = sum(jnp.dot(chosen, piece, preferred_element_type=f32) for piece in pieces)
        where = pl.ds(pl.multiple_of(image * share, share), share)
        placed_ref[:, where, :] = placed.reshape(shares, share, width)
        return 0

    lax.fori_loop(0, images, one_image, 0, unroll=2)


def total_body(parts_ref, out_ref):
    out_ref[...] = jnp.sum(parts_ref[...], axis=0)


def everyones(copies, axis):
    return lax.all_to_all(copies, axis, 0, 0, tiled=True)


def send_rows(values, to):
    return lax.ppermute(values, "rows", [(i, to(i)) for i in range(lax.axis_size("rows"))])


def local(student_patches, teacher_patches, mask_index, student_weight, teacher_weight):
    images, patches, depth = student_patches.shape
    masked = mask_index.shape[1]
    rows = images * masked
    row_devices = lax.axis_size("rows")
    proto_devices = lax.axis_size("protos")
    total_rows = float(rows * row_devices)
    protos = student_weight.shape[1]
    work = 2 * rows * protos * depth

    teacher_exp, column_part, student_exp, student_part, unit, inverse, turned, unit_weight, length = call(
        first_body,
        [
            ((rows, protos), f32),
            ((row_devices, 1, protos), f32),
            ((rows, protos), f32),
            ((1, rows), f32),
            ((rows, depth), f32),
            ((rows, LANES), f32),
            ((depth, rows), bf16),
            ((depth, protos), bf16),
            ((1, protos), f32),
        ],
        (teacher_patches, teacher_weight, student_patches, student_weight, mask_index),
        [
            pltpu.VMEM(teacher_patches.shape, bf16),
            pltpu.VMEM(teacher_weight.shape, bf16),
            pltpu.VMEM(student_patches.shape, bf16),
            pltpu.VMEM(student_weight.shape, bf16),
            pltpu.VMEM(mask_index.shape, jnp.int32),
            pltpu.VMEM((rows, depth), bf16),
            pltpu.VMEM((rows, depth), bf16),
            pltpu.VMEM((rows, LANES), f32),
            pltpu.SemaphoreType.DMA((5,)),
        ],
        limit=12, hbm=5, flops=2 * work, moved=2**23,
    )
    rider = student_part
    for sweep in range(SK_ITERS):
        column_sums = everyones(column_part, "rows")
        riders = [rider] if sweep < 2 else []
        col_scale, row_part = call(
            columns_body,
            [((1, protos), f32), ((proto_devices, 1, rows + LANES * len(riders)), f32)],
            (column_sums, teacher_exp, *riders),
            [pltpu.VMEM((rows, LANES), f32)],
            flops=2 * rows * protos, moved=2**23,
        )
        row_sums = everyones(row_part, "protos")
        if sweep == 1:
            student_sums = row_sums
        if sweep < SK_ITERS - 1:
            column_part, *riding = call(
                functools.partial(rows_body, total_rows),
                [((row_devices, 1, protos), f32)] + [((1, LANES), f32)] * (sweep == 0),
                (row_sums, teacher_exp),
                [pltpu.VMEM((rows, LANES), f32), pltpu.VMEM((8, protos), f32)],
                flops=2 * rows * protos, moved=2**23,
            )
            if sweep == 0:
                (rider,) = riding
    share = patches // proto_devices
    levels = row_devices // 2
    placed, mine, other = call(
        functools.partial(gradient_body, total_rows),
        [((proto_devices, images * share, depth), f32)]
        + [((levels, depth // row_devices, protos), f32)] * 2,
        (
            row_sums, student_sums, col_scale, teacher_exp, student_exp, unit_weight, turned, unit, inverse, mask_index,
            student_weight, length,
        ),
        [
            pltpu.VMEM((rows, LANES), f32),
            pltpu.VMEM((rows, LANES), f32),
            pltpu.VMEM((rows, depth), f32),
            pltpu.VMEM((rows, protos), bf16),
        ],
        limit=12, flops=2 * work, moved=2**24,
    )
    parts = mine + send_rows(other, lambda i: i ^ 1)
    grad_weight = parts[0]
    for ahead in range(1, levels):
        grad_weight = grad_weight + send_rows(parts[ahead], lambda i: (i + 2 * ahead) % row_devices)
    arrived = everyones(placed, "protos")
    (grad_patches,) = call(total_body, [(arrived.shape[1:], f32)], (arrived,))
    return (grad_patches.reshape(images, share, depth), grad_weight)


def solution(mesh):
    placed = (
        P("rows", None, None),
        P("rows", None, None),
        P("rows", None),
        P(None, "protos"),
        P(None, "protos"),
    )
    return jax.shard_map(
        local,
        mesh=mesh,
        in_specs=placed,
        out_specs=(P("rows", "protos", None), P("rows", "protos")),
        check_vma=False,
    )
```

```python
import functools
import math

import jax
import jax.numpy as jnp
from jax import lax
from jax.experimental import pallas as pl
from jax.experimental.pallas import tpu as pltpu
from jax.sharding import PartitionSpec as P

PROTOS = 65536
SK_ITERS = 3
LANES = 128

epsilon = 1e-06
temp_student = 0.1
temp_teacher = 0.07

f32 = jnp.float32
bf16 = jnp.bfloat16


def call(body, outs, ins, scratch=(), limit=8, hbm=0, flops=0, moved=0):
    held = [pltpu.with_memory_space_constraint(array, pltpu.HBM) for array in ins[:hbm]]
    spaces = [pltpu.HBM] * hbm + [pltpu.VMEM] * (len(ins) - hbm)
    return pl.pallas_call(
        body,
        out_shape=[
            (space[0] if space else pltpu.VMEM)(shape, dtype) for shape, dtype, *space in outs
        ],
        in_specs=[pl.BlockSpec(memory_space=space) for space in spaces],
        out_specs=[
            pl.BlockSpec(memory_space=pltpu.HBM if space and space[0] is pltpu.HBM else pltpu.VMEM)
            for _, _, *space in outs
        ],
        scratch_shapes=list(scratch),
        compiler_params=pltpu.CompilerParams(vmem_limit_bytes=limit * 2**20),
        cost_estimate=pl.CostEstimate(flops=flops, bytes_accessed=moved, transcendentals=0),
    )(*held, *ins[hbm:])


def pick(patches_ref, positions, image):
    patches = patches_ref.shape[1]
    masked = positions.shape[0]
    column = lax.broadcasted_iota(jnp.int32, (masked, patches), 1).astype(f32)
    chosen = (column == positions[:, image : image + 1]).astype(bf16)
    return jnp.dot(chosen, patches_ref[image], preferred_element_type=f32)


def lanes_of_rows(parts):
    groups = parts.shape[0] // LANES
    lane = lax.broadcasted_iota(jnp.int32, (LANES, LANES), 1)
    table = jnp.zeros((LANES, LANES), f32)
    for group in range(groups):
        column = jnp.sum(parts[group * LANES : (group + 1) * LANES], axis=1, keepdims=True)
        table = jnp.where(lane == group, column, table)
    table = table.T
    return jnp.concatenate([table[group : group + 1] for group in range(groups)], axis=1)


def fold_lanes(values):
    total = values[:, :LANES]
    for start in range(LANES, values.shape[1], LANES):
        total = total + values[:, start : start + LANES]
    return total


def rows_on_sublanes(line):
    pieces = [
        jnp.broadcast_to(line[:, s : s + LANES], (LANES, LANES)).T
        for s in range(0, line.shape[1], LANES)
    ]
    return jnp.concatenate(pieces, axis=0)


def spread(column, width):
    return jnp.concatenate([column] * (width // LANES), axis=1)


def unit_columns(weight_ref, cols):
    weight = weight_ref[:, cols].astype(f32)
    length = jnp.sqrt(jnp.sum(weight * weight, axis=0, keepdims=True) + epsilon)
    return weight * (1.0 / length), length


TILE = 256
LOG2_E = math.log2(math.e)


def first_body(
    teacher_hbm, teacher_weight_hbm, student_hbm, student_weight_hbm, mask_hbm,
    teacher_exp_ref, cols_ref, student_exp_ref, student_rows_ref, unit_ref, inverse_ref, turned_ref, unit_weight_ref,
    length_ref,
    teacher_ref, teacher_weight_ref, student_ref, student_weight_ref, mask_ref, teacher_bf_ref, student_bf_ref, parts_ref, sems,
):
    images, masked = mask_ref.shape
    protos = teacher_exp_ref.shape[1]
    loads = [
        pltpu.make_async_copy(source, target, sems.at[index])
        for index, (source, target) in enumerate(
            (
                (mask_hbm, mask_ref),
                (teacher_hbm, teacher_ref),
                (teacher_weight_hbm, teacher_weight_ref),
                (student_hbm, student_ref),
                (student_weight_hbm, student_weight_ref),
            )
        )
    ]
    for load in loads:
        load.start()
    loads[0].wait()
    positions = mask_ref[...].astype(f32).T
    loads[1].wait()
    for image in range(images):
        picked = pick(teacher_ref, positions, image)
        length = jnp.sqrt(jnp.sum(picked * picked, axis=1, keepdims=True) + epsilon)
        rows = slice(image * masked, (image + 1) * masked)
        teacher_bf_ref[rows, :] = (picked * (1.0 / length)).astype(bf16)
    loads[2].wait()

    def teacher_tile(tile, _):
        cols = pl.ds(pl.multiple_of(tile * TILE, TILE), TILE)
        unit = unit_columns(teacher_weight_ref, cols)[0].astype(bf16)
        products = jnp.dot(teacher_bf_ref[...], unit, preferred_element_type=f32)
        exps = jnp.exp2(products * (LOG2_E / temp_teacher))
        teacher_exp_ref[:, cols] = exps
        line = jnp.sum(exps, axis=0, keepdims=True)
        cols_ref[:, :, cols] = jnp.broadcast_to(line[None], (cols_ref.shape[0], 1, TILE))
        return 0

    lax.fori_loop(0, protos // TILE, teacher_tile, 0, unroll=4)
    loads[3].wait()

    for image in range(images):
        picked = pick(student_ref, positions, image)
        inverse = 1.0 / jnp.sqrt(jnp.sum(picked * picked, axis=1, keepdims=True) + epsilon)
        unit = picked * inverse
        rows = slice(image * masked, (image + 1) * masked)
        unit_ref[rows, :] = unit
        student_bf_ref[rows, :] = unit.astype(bf16)
        turned_ref[:, rows] = unit.T.astype(bf16)
        inverse_ref[rows, :] = jnp.broadcast_to(inverse, (masked, LANES))
    parts_ref[...] = jnp.zeros_like(parts_ref)
    loads[4].wait()

    def student_tile(tile, _):
        cols = pl.ds(pl.multiple_of(tile * TILE, TILE), TILE)
        unit, length = unit_columns(student_weight_ref, cols)
        length_ref[:, cols] = length
        unit = unit.astype(bf16)
        unit_weight_ref[:, cols] = unit
        products = jnp.dot(student_bf_ref[...], unit, preferred_element_type=f32)
        exps = jnp.exp2(products * (LOG2_E / temp_student))
        student_exp_ref[:, cols] = exps
        parts_ref[...] += fold_lanes(exps)
        return 0

    lax.fori_loop(0, protos // TILE, student_tile, 0, unroll=4)
    student_rows_ref[...] = lanes_of_rows(parts_ref[...])


def store_copies(out_ref, line):
    out_ref[...] = jnp.broadcast_to(line[None], out_ref.shape)


def columns_body(sums_ref, exp_ref, *refs):
    *rider, scale_ref, rows_ref, parts_ref = refs
    scale = 1.0 / (jnp.sum(sums_ref[...], axis=0) * PROTOS)
    scale_ref[...] = scale
    step = 64

    def block(index, _):
        rows = pl.ds(pl.multiple_of(index * step, step), step)
        total = exp_ref[rows, :LANES] * scale[:, :LANES]
        for start in range(LANES, exp_ref.shape[1], LANES):
            total = total + exp_ref[rows, start : start + LANES] * scale[:, start : start + LANES]
        parts_ref[rows, :] = total
        return 0

    lax.fori_loop(0, exp_ref.shape[0] // step, block, 0, unroll=2)
    line = lanes_of_rows(parts_ref[...])
    peers, _, width = rows_ref.shape
    rows = line.shape[1]
    rows_ref[:, :, :rows] = jnp.broadcast_to(line[None], (peers, 1, rows))
    if rider:
        groups = rider[0].shape[1] // LANES
        for group in range(groups):
            lanes = rider[0][:, group * LANES : (group + 1) * LANES]
            some = slice(group * peers // groups, (group + 1) * peers // groups)
            rows_ref[some, :, rows:] = jnp.broadcast_to(lanes[None], (peers // groups, 1, LANES))


def rows_body(total_rows, sums_ref, exp_ref, cols_ref, *refs):
    *rider, scale_ref, parts_ref = refs
    sums = jnp.sum(sums_ref[...], axis=0)
    line = 1.0 / (sums[:, : exp_ref.shape[0]] * total_rows)
    if rider:
        rider[0][...] = sums[:, exp_ref.shape[0] :]
    scale_ref[...] = rows_on_sublanes(line)
    width = exp_ref.shape[1]
    parts_ref[...] = jnp.zeros_like(parts_ref)
    step = 64

    def block(index, _):
        rows = pl.ds(pl.multiple_of(index * step, step), step)
        scale = scale_ref[rows, :]
        for start in range(0, width, LANES):
            product = exp_ref[rows, start : start + LANES] * scale
            total = product[0:8]
            for r in range(8, step, 8):
                total = total + product[r : r + 8]
            parts_ref[:, start : start + LANES] += total
        return 0

    lax.fori_loop(0, exp_ref.shape[0] // step, block, 0, unroll=2)
    store_copies(cols_ref, jnp.sum(parts_ref[...], axis=0, keepdims=True))


def three_pieces(values):
    high = values.astype(bf16)
    rest = values - high.astype(f32)
    middle = rest.astype(bf16)
    return high, middle, (rest - middle.astype(f32)).astype(bf16)


def feature_body(
    total_rows,
    sums_ref, student_ref, cols_ref, teacher_exp_ref, student_exp_ref, unit_weight_ref, unit_ref, inverse_ref,
    mask_ref,
    placed_ref, score_hbm, row_ref, total_ref, sum_ref, score_ref, sem,
):
    rows = teacher_exp_ref.shape[0]
    row_ref[...] = rows_on_sublanes(1.0 / (jnp.sum(sums_ref[...], axis=0) * total_rows))
    groups = rows // LANES
    step = student_ref.shape[0] // groups
    totals = jnp.concatenate([student_ref[group * step][:, rows:] for group in range(groups)], axis=1)
    total_ref[...] = rows_on_sublanes((1.0 / temp_student) / totals)

    def one_tile(tile, _):
        cols = pl.ds(pl.multiple_of(tile * TILE, TILE), TILE)
        target = teacher_exp_ref[:, cols] * spread(row_ref[...], TILE)
        target = target * (cols_ref[:, cols] * (total_rows / temp_student))
        score = (student_exp_ref[:, cols] * spread(total_ref[...], TILE) - target).astype(bf16)
        score_ref[:, cols] = score
        return 0

    lax.fori_loop(0, teacher_exp_ref.shape[1] // TILE, one_tile, 0, unroll=2)
    store = pltpu.make_async_copy(score_ref, score_hbm, sem)
    store.start()
    sum_ref[...] = lax.dot_general(
        score_ref[...], unit_weight_ref[...], (((1,), (1,)), ((), ())), preferred_element_type=f32
    )
    images, masked = mask_ref.shape
    width = unit_ref.shape[1]
    shares = placed_ref.shape[0]
    share = placed_ref.shape[1] // images
    patch = lax.broadcasted_iota(jnp.int32, (shares * share, masked), 0)

    def one_image(image, _):
        rows = pl.ds(pl.multiple_of(image * masked, masked), masked)
        unit = unit_ref[rows, :]
        total = sum_ref[rows, :]
        projection = jnp.sum(unit * total, axis=1, keepdims=True)
        pieces = three_pieces((total - unit * projection) * spread(inverse_ref[rows, :], width))
        chosen = (patch == mask_ref[pl.ds(image, 1), :]).astype(bf16)
        placed = sum(jnp.dot(chosen, piece, preferred_element_type=f32) for piece in pieces)
        where = pl.ds(pl.multiple_of(image * share, share), share)
        placed_ref[:, where, :] = placed.reshape(shares, share, width)
        return 0

    lax.fori_loop(0, images, one_image, 0, unroll=2)
    store.wait()


def weight_body(
    score_hbm, weight_hbm, turned_ref, length_ref, mine_ref, other_ref, score_ref, weight_ref, sems
):
    levels, share = mine_ref.shape[:2]
    me = lax.axis_index("rows")
    core, level = me % 2, me // 2
    tiles = weight_ref.shape[1] // TILE
    weight_load = pltpu.make_async_copy(weight_hbm, weight_ref, sems.at[tiles])
    weight_load.start()
    loads = [
        pltpu.make_async_copy(
            score_hbm.at[:, pl.ds(tile * TILE, TILE)], score_ref.at[:, pl.ds(tile * TILE, TILE)], sems.at[tile]
        )
        for tile in range(tiles)
    ]
    for load in loads:
        load.start()
    weight_load.wait()
    for tile in range(tiles):
        cols = slice(tile * TILE, (tile + 1) * TILE)
        loads[tile].wait()
        total = jnp.dot(turned_ref[...], score_ref[:, cols], preferred_element_type=f32)
        inverse = 1.0 / length_ref[:, cols]
        unit = weight_ref[:, cols].astype(f32) * inverse
        dots = jnp.sum(unit * total, axis=0, keepdims=True)
        gradient = ((total - unit * dots) * inverse).reshape(levels, 2, share, TILE)
        for z in range(levels):
            place = pl.ds((z + levels - level) % levels, 1)
            mine_ref[place, :, cols] = jnp.where(core == 0, gradient[z, 0], gradient[z, 1])[None]
            other_ref[place, :, cols] = jnp.where(core == 0, gradient[z, 1], gradient[z, 0])[None]


def total_body(parts_hbm, out_ref, parts_ref, sems):
    pieces = sems.shape[0]
    size = parts_ref.shape[0] // pieces
    loads = [
        pltpu.make_async_copy(
            parts_hbm.at[pl.ds(piece * size, size)], parts_ref.at[pl.ds(piece * size, size)], sems.at[piece]
        )
        for piece in range(pieces)
    ]
    for load in loads:
        load.start()
    total = None
    for piece in range(pieces):
        loads[piece].wait()
        part = jnp.sum(parts_ref[piece * size : (piece + 1) * size], axis=0)
        total = part if total is None else total + part
    out_ref[...] = total


def everyones(copies, axis):
    return lax.all_to_all(copies, axis, 0, 0, tiled=True)


def send_rows(values, to):
    return lax.ppermute(values, "rows", [(i, to(i)) for i in range(lax.axis_size("rows"))])


def ring_share(parts, levels):
    def along(values, by):
        return send_rows(values, lambda i: (i + 2 * by) % (2 * levels))

    last = levels // 2
    total = parts[0]
    if levels > 1:
        up = parts[last]
        for k in range(last - 1, 0, -1):
            up = along(up, 1) + parts[k]
        total = total + along(up, 1)
    if levels > 2:
        down = parts[last + 1]
        for k in range(last + 2, levels):
            down = along(down, -1) + parts[k]
        total = total + along(down, -1)
    return total


def local(student_patches, teacher_patches, mask_index, student_weight, teacher_weight):
    images, patches, depth = student_patches.shape
    masked = mask_index.shape[1]
    rows = images * masked
    row_devices = lax.axis_size("rows")
    proto_devices = lax.axis_size("protos")
    total_rows = float(rows * row_devices)
    protos = student_weight.shape[1]
    work = 2 * rows * protos * depth

    teacher_exp, column_part, student_exp, student_part, unit, inverse, turned, unit_weight, length = call(
        first_body,
        [
            ((rows, protos), f32),
            ((row_devices, 1, protos), f32),
            ((rows, protos), f32),
            ((1, rows), f32),
            ((rows, depth), f32),
            ((rows, LANES), f32),
            ((depth, rows), bf16),
            ((depth, protos), bf16),
            ((1, protos), f32),
        ],
        (teacher_patches, teacher_weight, student_patches, student_weight, mask_index),
        [
            pltpu.VMEM(teacher_patches.shape, bf16),
            pltpu.VMEM(teacher_weight.shape, bf16),
            pltpu.VMEM(student_patches.shape, bf16),
            pltpu.VMEM(student_weight.shape, bf16),
            pltpu.VMEM(mask_index.shape, jnp.int32),
            pltpu.VMEM((rows, depth), bf16),
            pltpu.VMEM((rows, depth), bf16),
            pltpu.VMEM((rows, LANES), f32),
            pltpu.SemaphoreType.DMA((5,)),
        ],
        limit=12, hbm=5, flops=2 * work, moved=2**23,
    )
    rider = student_part
    for sweep in range(SK_ITERS):
        column_sums = everyones(column_part, "rows")
        riders = [rider] if sweep < 2 else []
        col_scale, row_part = call(
            columns_body,
            [((1, protos), f32), ((proto_devices, 1, rows + LANES * len(riders)), f32)],
            (column_sums, teacher_exp, *riders),
            [pltpu.VMEM((rows, LANES), f32)],
            flops=2 * rows * protos, moved=2**23,
        )
        row_sums = everyones(row_part, "protos")
        if sweep == 1:
            student_sums = row_sums
        if sweep < SK_ITERS - 1:
            column_part, *riding = call(
                functools.partial(rows_body, total_rows),
                [((row_devices, 1, protos), f32)] + [((1, LANES), f32)] * (sweep == 0),
                (row_sums, teacher_exp),
                [pltpu.VMEM((rows, LANES), f32), pltpu.VMEM((8, protos), f32)],
                flops=2 * rows * protos, moved=2**23,
            )
            if sweep == 0:
                (rider,) = riding
    share = patches // proto_devices
    levels = row_devices // 2
    placed, score = call(
        functools.partial(feature_body, total_rows),
        [((proto_devices, images * share, depth), f32), ((rows, protos), bf16, pltpu.HBM)],
        (row_sums, student_sums, col_scale, teacher_exp, student_exp, unit_weight, unit, inverse, mask_index),
        [
            pltpu.VMEM((rows, LANES), f32),
            pltpu.VMEM((rows, LANES), f32),
            pltpu.VMEM((rows, depth), f32),
            pltpu.VMEM((rows, protos), bf16),
            pltpu.SemaphoreType.DMA,
        ],
        limit=12, flops=work, moved=2**24,
    )
    arrived = everyones(placed, "protos")
    mine, other = call(
        weight_body,
        [((levels, depth // row_devices, protos), f32)] * 2,
        (score, student_weight, turned, length),
        [
            pltpu.VMEM((rows, protos), bf16),
            pltpu.VMEM(student_weight.shape, bf16),
            pltpu.SemaphoreType.DMA((protos // TILE + 1,)),
        ],
        limit=12, hbm=2,
    )
    grad_weight = ring_share(mine + send_rows(other, lambda i: i ^ 1), levels)
    (grad_patches,) = call(
        total_body,
        [(arrived.shape[1:], f32, jax.ShapeDtypeStruct)],
        (arrived,),
        [pltpu.VMEM(arrived.shape, f32), pltpu.SemaphoreType.DMA((4 if proto_devices % 4 == 0 else 1,))],
        hbm=1,
    )
    return (grad_patches.reshape(images, share, depth), grad_weight)


def solution(mesh):
    placed = (
        P("rows", None, None),
        P("rows", None, None),
        P("rows", None),
        P(None, "protos"),
        P(None, "protos"),
    )
    return jax.shard_map(
        local,
        mesh=mesh,
        in_specs=placed,
        out_specs=(P("rows", "protos", None), P("rows", "protos")),
        check_vma=False,
    )
```

```python
import functools
import math

import jax
import jax.numpy as jnp
from jax import lax
from jax.experimental import pallas as pl
from jax.experimental.pallas import tpu as pltpu
from jax.sharding import PartitionSpec as P

PROTOS = 65536
SK_ITERS = 3
LANES = 128

epsilon = 1e-06
temp_student = 0.1
temp_teacher = 0.07

f32 = jnp.float32
bf16 = jnp.bfloat16


def call(body, outs, ins, scratch=(), limit=8, hbm=0, flops=0, moved=0):
    held = [pltpu.with_memory_space_constraint(array, pltpu.HBM) for array in ins[:hbm]]
    spaces = [pltpu.HBM] * hbm + [pltpu.VMEM] * (len(ins) - hbm)
    return pl.pallas_call(
        body,
        out_shape=[
            (space[0] if space else pltpu.VMEM)(shape, dtype) for shape, dtype, *space in outs
        ],
        in_specs=[pl.BlockSpec(memory_space=space) for space in spaces],
        out_specs=[
            pl.BlockSpec(memory_space=pltpu.HBM if space and space[0] is pltpu.HBM else pltpu.VMEM)
            for _, _, *space in outs
        ],
        scratch_shapes=list(scratch),
        compiler_params=pltpu.CompilerParams(vmem_limit_bytes=limit * 2**20),
        cost_estimate=pl.CostEstimate(flops=flops, bytes_accessed=moved, transcendentals=0),
    )(*held, *ins[hbm:])


def pick(patches_ref, positions, image):
    patches = patches_ref.shape[1]
    masked = positions.shape[0]
    column = lax.broadcasted_iota(jnp.int32, (masked, patches), 1).astype(f32)
    chosen = (column == positions[:, image : image + 1]).astype(bf16)
    return jnp.dot(chosen, patches_ref[image], preferred_element_type=f32)


def lanes_of_rows(parts):
    groups = parts.shape[0] // LANES
    lane = lax.broadcasted_iota(jnp.int32, (LANES, LANES), 1)
    table = jnp.zeros((LANES, LANES), f32)
    for group in range(groups):
        column = jnp.sum(parts[group * LANES : (group + 1) * LANES], axis=1, keepdims=True)
        table = jnp.where(lane == group, column, table)
    table = table.T
    return jnp.concatenate([table[group : group + 1] for group in range(groups)], axis=1)


def fold_lanes(values):
    total = values[:, :LANES]
    for start in range(LANES, values.shape[1], LANES):
        total = total + values[:, start : start + LANES]
    return total


def rows_on_sublanes(line):
    pieces = [
        jnp.broadcast_to(line[:, s : s + LANES], (LANES, LANES)).T
        for s in range(0, line.shape[1], LANES)
    ]
    return jnp.concatenate(pieces, axis=0)


def spread(column, width):
    return jnp.concatenate([column] * (width // LANES), axis=1)


def unit_columns(weight_ref, cols):
    weight = weight_ref[:, cols].astype(f32)
    length = jnp.sqrt(jnp.sum(weight * weight, axis=0, keepdims=True) + epsilon)
    return weight * (1.0 / length), length


TILE = 256
LOG2_E = math.log2(math.e)


def first_body(
    teacher_hbm, teacher_weight_hbm, student_hbm, student_weight_hbm, mask_hbm,
    teacher_exp_ref, cols_ref, student_exp_ref, student_rows_ref, unit_ref, inverse_ref, turned_ref, unit_weight_ref,
    length_ref,
    teacher_ref, teacher_weight_ref, student_ref, student_weight_ref, mask_ref, teacher_bf_ref, student_bf_ref, parts_ref, sems,
):
    images, masked = mask_ref.shape
    protos = teacher_exp_ref.shape[1]
    loads = [
        pltpu.make_async_copy(source, target, sems.at[index])
        for index, (source, target) in enumerate(
            (
                (mask_hbm, mask_ref),
                (teacher_hbm, teacher_ref),
                (teacher_weight_hbm, teacher_weight_ref),
                (student_hbm, student_ref),
                (student_weight_hbm, student_weight_ref),
            )
        )
    ]
    for load in loads:
        load.start()
    loads[0].wait()
    positions = mask_ref[...].astype(f32).T
    loads[1].wait()
    for image in range(images):
        picked = pick(teacher_ref, positions, image)
        length = jnp.sqrt(jnp.sum(picked * picked, axis=1, keepdims=True) + epsilon)
        rows = slice(image * masked, (image + 1) * masked)
        teacher_bf_ref[rows, :] = (picked * (1.0 / length)).astype(bf16)
    loads[2].wait()

    def teacher_tile(tile, _):
        cols = pl.ds(pl.multiple_of(tile * TILE, TILE), TILE)
        unit = unit_columns(teacher_weight_ref, cols)[0].astype(bf16)
        products = jnp.dot(teacher_bf_ref[...], unit, preferred_element_type=f32)
        exps = jnp.exp2(products * (LOG2_E / temp_teacher))
        teacher_exp_ref[:, cols] = exps
        line = jnp.sum(exps, axis=0, keepdims=True)
        cols_ref[:, :, cols] = jnp.broadcast_to(line[None], (cols_ref.shape[0], 1, TILE))
        return 0

    lax.fori_loop(0, protos // TILE, teacher_tile, 0, unroll=4)
    loads[3].wait()

    for image in range(images):
        picked = pick(student_ref, positions, image)
        inverse = 1.0 / jnp.sqrt(jnp.sum(picked * picked, axis=1, keepdims=True) + epsilon)
        unit = picked * inverse
        rows = slice(image * masked, (image + 1) * masked)
        unit_ref[rows, :] = unit
        student_bf_ref[rows, :] = unit.astype(bf16)
        turned_ref[:, rows] = unit.T.astype(bf16)
        inverse_ref[rows, :] = jnp.broadcast_to(inverse, (masked, LANES))
    parts_ref[...] = jnp.zeros_like(parts_ref)
    loads[4].wait()

    def student_tile(tile, _):
        cols = pl.ds(pl.multiple_of(tile * TILE, TILE), TILE)
        unit, length = unit_columns(student_weight_ref, cols)
        length_ref[:, cols] = length
        unit = unit.astype(bf16)
        unit_weight_ref[:, cols] = unit
        products = jnp.dot(student_bf_ref[...], unit, preferred_element_type=f32)
        exps = jnp.exp2(products * (LOG2_E / temp_student))
        student_exp_ref[:, cols] = exps
        parts_ref[...] += fold_lanes(exps)
        return 0

    lax.fori_loop(0, protos // TILE, student_tile, 0, unroll=4)
    student_rows_ref[...] = lanes_of_rows(parts_ref[...])


def store_copies(out_ref, line):
    out_ref[...] = jnp.broadcast_to(line[None], out_ref.shape)


def columns_body(sums_ref, exp_ref, *refs):
    *rider, scale_ref, rows_ref, parts_ref = refs
    scale = 1.0 / (jnp.sum(sums_ref[...], axis=0) * PROTOS)
    scale_ref[...] = scale
    step = 64

    def block(index, _):
        rows = pl.ds(pl.multiple_of(index * step, step), step)
        total = exp_ref[rows, :LANES] * scale[:, :LANES]
        for start in range(LANES, exp_ref.shape[1], LANES):
            total = total + exp_ref[rows, start : start + LANES] * scale[:, start : start + LANES]
        parts_ref[rows, :] = total
        return 0

    lax.fori_loop(0, exp_ref.shape[0] // step, block, 0, unroll=2)
    line = lanes_of_rows(parts_ref[...])
    peers, _, width = rows_ref.shape
    rows = line.shape[1]
    rows_ref[:, :, :rows] = jnp.broadcast_to(line[None], (peers, 1, rows))
    if rider:
        groups = rider[0].shape[1] // LANES
        for group in range(groups):
            lanes = rider[0][:, group * LANES : (group + 1) * LANES]
            some = slice(group * peers // groups, (group + 1) * peers // groups)
            rows_ref[some, :, rows:] = jnp.broadcast_to(lanes[None], (peers // groups, 1, LANES))


def rows_body(total_rows, sums_ref, exp_ref, cols_ref, *refs):
    *rider, scale_ref, parts_ref = refs
    sums = jnp.sum(sums_ref[...], axis=0)
    line = 1.0 / (sums[:, : exp_ref.shape[0]] * total_rows)
    if rider:
        rider[0][...] = sums[:, exp_ref.shape[0] :]
    scale_ref[...] = rows_on_sublanes(line)
    width = exp_ref.shape[1]
    parts_ref[...] = jnp.zeros_like(parts_ref)
    step = 64

    def block(index, _):
        rows = pl.ds(pl.multiple_of(index * step, step), step)
        scale = scale_ref[rows, :]
        for start in range(0, width, LANES):
            product = exp_ref[rows, start : start + LANES] * scale
            total = product[0:8]
            for r in range(8, step, 8):
                total = total + product[r : r + 8]
            parts_ref[:, start : start + LANES] += total
        return 0

    lax.fori_loop(0, exp_ref.shape[0] // step, block, 0, unroll=2)
    store_copies(cols_ref, jnp.sum(parts_ref[...], axis=0, keepdims=True))


def feature_body(
    total_rows,
    sums_ref, student_ref, cols_ref, teacher_exp_ref, student_exp_ref, unit_weight_ref, unit_ref, inverse_ref,
    mask_ref,
    placed_ref, score_hbm, row_ref, total_ref, sum_ref, score_ref, sem,
):
    rows = teacher_exp_ref.shape[0]
    row_ref[...] = rows_on_sublanes(1.0 / (jnp.sum(sums_ref[...], axis=0) * total_rows))
    groups = rows // LANES
    step = student_ref.shape[0] // groups
    totals = jnp.concatenate([student_ref[group * step][:, rows:] for group in range(groups)], axis=1)
    total_ref[...] = rows_on_sublanes((1.0 / temp_student) / totals)

    def one_tile(tile, _):
        cols = pl.ds(pl.multiple_of(tile * TILE, TILE), TILE)
        target = teacher_exp_ref[:, cols] * spread(row_ref[...], TILE)
        target = target * (cols_ref[:, cols] * (total_rows / temp_student))
        score = (student_exp_ref[:, cols] * spread(total_ref[...], TILE) - target).astype(bf16)
        score_ref[:, cols] = score
        return 0

    lax.fori_loop(0, teacher_exp_ref.shape[1] // TILE, one_tile, 0, unroll=2)
    store = pltpu.make_async_copy(score_ref, score_hbm, sem)
    store.start()
    sum_ref[...] = lax.dot_general(
        score_ref[...], unit_weight_ref[...], (((1,), (1,)), ((), ())), preferred_element_type=f32
    )
    images, masked = mask_ref.shape
    width = unit_ref.shape[1]
    shares = placed_ref.shape[0]
    share = placed_ref.shape[1] // images
    patch = lax.broadcasted_iota(jnp.int32, (shares * share, 2 * masked), 0)

    def one_image(image, _):
        rows = pl.ds(pl.multiple_of(image * masked, masked), masked)
        unit = unit_ref[rows, :]
        total = sum_ref[rows, :]
        projection = jnp.sum(unit * total, axis=1, keepdims=True)
        gradient = (total - unit * projection) * spread(inverse_ref[rows, :], width)
        high = gradient.astype(bf16)
        low = (gradient - high.astype(f32)).astype(bf16)
        positions = mask_ref[pl.ds(image, 1), :]
        chosen = (patch == jnp.concatenate([positions, positions], axis=1)).astype(bf16)
        placed = jnp.dot(chosen, jnp.concatenate([high, low], axis=0), preferred_element_type=f32)
        where = pl.ds(pl.multiple_of(image * share, share), share)
        placed_ref[:, where, :] = placed.reshape(shares, share, width)
        return 0

    lax.fori_loop(0, images, one_image, 0, unroll=4)
    store.wait()


def weight_body(
    score_hbm, weight_hbm, turned_ref, length_ref, mine_ref, other_ref, score_ref, weight_ref, sems
):
    levels, share = mine_ref.shape[:2]
    me = lax.axis_index("rows")
    core, level = me % 2, me // 2
    tiles = weight_ref.shape[1] // TILE
    weight_load = pltpu.make_async_copy(weight_hbm, weight_ref, sems.at[tiles])
    weight_load.start()
    loads = [
        pltpu.make_async_copy(
            score_hbm.at[:, pl.ds(tile * TILE, TILE)], score_ref.at[:, pl.ds(tile * TILE, TILE)], sems.at[tile]
        )
        for tile in range(tiles)
    ]
    for load in loads:
        load.start()
    weight_load.wait()
    for tile in range(tiles):
        cols = slice(tile * TILE, (tile + 1) * TILE)
        loads[tile].wait()
        total = jnp.dot(turned_ref[...], score_ref[:, cols], preferred_element_type=f32)
        inverse = 1.0 / length_ref[:, cols]
        unit = weight_ref[:, cols].astype(f32) * inverse
        dots = jnp.sum(unit * total, axis=0, keepdims=True)
        gradient = ((total - unit * dots) * inverse).reshape(levels, 2, share, TILE)
        for z in range(levels):
            place = pl.ds((z + levels - level) % levels, 1)
            mine_ref[place, :, cols] = jnp.where(core == 0, gradient[z, 0], gradient[z, 1])[None]
            other_ref[place, :, cols] = jnp.where(core == 0, gradient[z, 1], gradient[z, 0])[None]


def total_body(parts_ref, out_ref):
    out_ref[...] = jnp.sum(parts_ref[...], axis=0)


def everyones(copies, axis):
    return lax.all_to_all(copies, axis, 0, 0, tiled=True)


def send_rows(values, to):
    return lax.ppermute(values, "rows", [(i, to(i)) for i in range(lax.axis_size("rows"))])


def ring_share(parts, levels):
    def along(values, by):
        return send_rows(values, lambda i: (i + 2 * by) % (2 * levels))

    last = levels // 2
    total = parts[0]
    if levels > 1:
        up = parts[last]
        for k in range(last - 1, 0, -1):
            up = along(up, 1) + parts[k]
        total = total + along(up, 1)
    if levels > 2:
        down = parts[last + 1]
        for k in range(last + 2, levels):
            down = along(down, -1) + parts[k]
        total = total + along(down, -1)
    return total


def local(student_patches, teacher_patches, mask_index, student_weight, teacher_weight):
    images, patches, depth = student_patches.shape
    masked = mask_index.shape[1]
    rows = images * masked
    row_devices = lax.axis_size("rows")
    proto_devices = lax.axis_size("protos")
    total_rows = float(rows * row_devices)
    protos = student_weight.shape[1]
    work = 2 * rows * protos * depth

    teacher_exp, column_part, student_exp, student_part, unit, inverse, turned, unit_weight, length = call(
        first_body,
        [
            ((rows, protos), f32),
            ((row_devices, 1, protos), f32),
            ((rows, protos), f32),
            ((1, rows), f32),
            ((rows, depth), f32),
            ((rows, LANES), f32),
            ((depth, rows), bf16),
            ((depth, protos), bf16),
            ((1, protos), f32),
        ],
        (teacher_patches, teacher_weight, student_patches, student_weight, mask_index),
        [
            pltpu.VMEM(teacher_patches.shape, bf16),
            pltpu.VMEM(teacher_weight.shape, bf16),
            pltpu.VMEM(student_patches.shape, bf16),
            pltpu.VMEM(student_weight.shape, bf16),
            pltpu.VMEM(mask_index.shape, jnp.int32),
            pltpu.VMEM((rows, depth), bf16),
            pltpu.VMEM((rows, depth), bf16),
            pltpu.VMEM((rows, LANES), f32),
            pltpu.SemaphoreType.DMA((5,)),
        ],
        limit=12, hbm=5, flops=2 * work, moved=2**23,
    )
    rider = student_part
    for sweep in range(SK_ITERS):
        column_sums = everyones(column_part, "rows")
        riders = [rider] if sweep < 2 else []
        col_scale, row_part = call(
            columns_body,
            [((1, protos), f32), ((proto_devices, 1, rows + LANES * len(riders)), f32)],
            (column_sums, teacher_exp, *riders),
            [pltpu.VMEM((rows, LANES), f32)],
            flops=2 * rows * protos, moved=2**23,
        )
        row_sums = everyones(row_part, "protos")
        if sweep == 1:
            student_sums = row_sums
        if sweep < SK_ITERS - 1:
            column_part, *riding = call(
                functools.partial(rows_body, total_rows),
                [((row_devices, 1, protos), f32)] + [((1, LANES), f32)] * (sweep == 0),
                (row_sums, teacher_exp),
                [pltpu.VMEM((rows, LANES), f32), pltpu.VMEM((8, protos), f32)],
                flops=2 * rows * protos, moved=2**23,
            )
            if sweep == 0:
                (rider,) = riding
    share = patches // proto_devices
    levels = row_devices // 2
    placed, score = call(
        functools.partial(feature_body, total_rows),
        [((proto_devices, images * share, depth), f32), ((rows, protos), bf16, pltpu.HBM)],
        (row_sums, student_sums, col_scale, teacher_exp, student_exp, unit_weight, unit, inverse, mask_index),
        [
            pltpu.VMEM((rows, LANES), f32),
            pltpu.VMEM((rows, LANES), f32),
            pltpu.VMEM((rows, depth), f32),
            pltpu.VMEM((rows, protos), bf16),
            pltpu.SemaphoreType.DMA,
        ],
        limit=12, flops=work, moved=2**24,
    )
    arrived = everyones(placed, "protos")
    mine, other = call(
        weight_body,
        [((levels, depth // row_devices, protos), f32)] * 2,
        (score, student_weight, turned, length),
        [
            pltpu.VMEM((rows, protos), bf16),
            pltpu.VMEM(student_weight.shape, bf16),
            pltpu.SemaphoreType.DMA((protos // TILE + 1,)),
        ],
        limit=12, hbm=2,
    )
    grad_weight = ring_share(mine + send_rows(other, lambda i: i ^ 1), levels)
    (grad_patches,) = call(
        total_body,
        [(arrived.shape[1:], f32, jax.ShapeDtypeStruct)],
        (arrived,),
    )
    return (grad_patches.reshape(images, share, depth), grad_weight)


def solution(mesh):
    placed = (
        P("rows", None, None),
        P("rows", None, None),
        P("rows", None),
        P(None, "protos"),
        P(None, "protos"),
    )
    return jax.shard_map(
        local,
        mesh=mesh,
        in_specs=placed,
        out_specs=(P("rows", "protos", None), P("rows", "protos")),
        check_vma=False,
    )
```

```python
import functools
import math

import jax
import jax.numpy as jnp
from jax import lax
from jax.experimental import pallas as pl
from jax.experimental.pallas import tpu as pltpu
from jax.sharding import PartitionSpec as P

PROTOS = 65536
SK_ITERS = 3
LANES = 128

epsilon = 1e-06
temp_student = 0.1
temp_teacher = 0.07

f32 = jnp.float32
bf16 = jnp.bfloat16


def call(body, outs, ins, scratch=(), limit=8, hbm=0, flops=0, moved=0):
    held = [pltpu.with_memory_space_constraint(array, pltpu.HBM) for array in ins[:hbm]]
    spaces = [pltpu.HBM] * hbm + [pltpu.VMEM] * (len(ins) - hbm)
    return pl.pallas_call(
        body,
        out_shape=[
            (space[0] if space else pltpu.VMEM)(shape, dtype) for shape, dtype, *space in outs
        ],
        in_specs=[pl.BlockSpec(memory_space=space) for space in spaces],
        out_specs=[
            pl.BlockSpec(memory_space=pltpu.HBM if space and space[0] is pltpu.HBM else pltpu.VMEM)
            for _, _, *space in outs
        ],
        scratch_shapes=list(scratch),
        compiler_params=pltpu.CompilerParams(vmem_limit_bytes=limit * 2**20),
        cost_estimate=pl.CostEstimate(flops=flops, bytes_accessed=moved, transcendentals=0),
    )(*held, *ins[hbm:])


def pick(patches_ref, positions, image):
    patches = patches_ref.shape[1]
    masked = positions.shape[0]
    column = lax.broadcasted_iota(jnp.int32, (masked, patches), 1).astype(f32)
    chosen = (column == positions[:, image : image + 1]).astype(bf16)
    return jnp.dot(chosen, patches_ref[image], preferred_element_type=f32)


def lanes_of_rows(parts):
    groups = parts.shape[0] // LANES
    lane = lax.broadcasted_iota(jnp.int32, (LANES, LANES), 1)
    table = jnp.zeros((LANES, LANES), f32)
    for group in range(groups):
        column = jnp.sum(parts[group * LANES : (group + 1) * LANES], axis=1, keepdims=True)
        table = jnp.where(lane == group, column, table)
    table = table.T
    return jnp.concatenate([table[group : group + 1] for group in range(groups)], axis=1)


def fold_lanes(values):
    total = values[:, :LANES]
    for start in range(LANES, values.shape[1], LANES):
        total = total + values[:, start : start + LANES]
    return total


def rows_on_sublanes(line):
    pieces = [
        jnp.broadcast_to(line[:, s : s + LANES], (LANES, LANES)).T
        for s in range(0, line.shape[1], LANES)
    ]
    return jnp.concatenate(pieces, axis=0)


def spread(column, width):
    return jnp.concatenate([column] * (width // LANES), axis=1)


def unit_columns(weight_ref, cols):
    weight = weight_ref[:, cols].astype(f32)
    length = jnp.sqrt(jnp.sum(weight * weight, axis=0, keepdims=True) + epsilon)
    return weight * (1.0 / length), length


TILE = 256
LOG2_E = math.log2(math.e)


def first_body(
    teacher_hbm, teacher_weight_hbm, student_hbm, student_weight_hbm, mask_hbm,
    teacher_exp_ref, cols_ref, student_exp_ref, student_rows_ref, unit_ref, inverse_ref, turned_ref, unit_weight_ref,
    length_ref,
    teacher_ref, teacher_weight_ref, student_ref, student_weight_ref, mask_ref, teacher_bf_ref, student_bf_ref, parts_ref, sems,
):
    images, masked = mask_ref.shape
    protos = teacher_exp_ref.shape[1]
    mask_load, teacher_weight_load, student_load, student_weight_load = [
        pltpu.make_async_copy(source, target, sems.at[index])
        for index, (source, target) in enumerate(
            (
                (mask_hbm, mask_ref),
                (teacher_weight_hbm, teacher_weight_ref),
                (student_hbm, student_ref),
                (student_weight_hbm, student_weight_ref),
            )
        )
    ]
    teacher_loads = [
        pltpu.make_async_copy(teacher_hbm.at[image], teacher_ref.at[image], sems.at[4 + image])
        for image in range(images)
    ]
    mask_load.start()
    for load in teacher_loads:
        load.start()
    teacher_weight_load.start()
    mask_load.wait()
    positions = mask_ref[...].astype(f32).T
    for image in range(images):
        teacher_loads[image].wait()
        picked = pick(teacher_ref, positions, image)
        length = jnp.sqrt(jnp.sum(picked * picked, axis=1, keepdims=True) + epsilon)
        rows = slice(image * masked, (image + 1) * masked)
        teacher_bf_ref[rows, :] = (picked * (1.0 / length)).astype(bf16)
    student_load.start()
    student_weight_load.start()
    teacher_weight_load.wait()

    def teacher_tile(tile, _):
        cols = pl.ds(pl.multiple_of(tile * TILE, TILE), TILE)
        unit = unit_columns(teacher_weight_ref, cols)[0].astype(bf16)
        products = jnp.dot(teacher_bf_ref[...], unit, preferred_element_type=f32)
        exps = jnp.exp2(products * (LOG2_E / temp_teacher))
        teacher_exp_ref[:, cols] = exps
        line = jnp.sum(exps, axis=0, keepdims=True)
        cols_ref[:, :, cols] = jnp.broadcast_to(line[None], (cols_ref.shape[0], 1, TILE))
        return 0

    lax.fori_loop(0, protos // TILE, teacher_tile, 0, unroll=4)
    student_load.wait()

    for image in range(images):
        picked = pick(student_ref, positions, image)
        inverse = 1.0 / jnp.sqrt(jnp.sum(picked * picked, axis=1, keepdims=True) + epsilon)
        unit = picked * inverse
        rows = slice(image * masked, (image + 1) * masked)
        unit_ref[rows, :] = unit
        student_bf_ref[rows, :] = unit.astype(bf16)
        turned_ref[:, rows] = unit.T.astype(bf16)
        inverse_ref[rows, :] = jnp.broadcast_to(inverse, (masked, LANES))
    parts_ref[...] = jnp.zeros_like(parts_ref)
    student_weight_load.wait()

    def student_tile(tile, _):
        cols = pl.ds(pl.multiple_of(tile * TILE, TILE), TILE)
        unit, length = unit_columns(student_weight_ref, cols)
        length_ref[:, cols] = length
        unit = unit.astype(bf16)
        unit_weight_ref[:, cols] = unit
        products = jnp.dot(student_bf_ref[...], unit, preferred_element_type=f32)
        exps = jnp.exp2(products * (LOG2_E / temp_student))
        student_exp_ref[:, cols] = exps
        parts_ref[...] += fold_lanes(exps)
        return 0

    lax.fori_loop(0, protos // TILE, student_tile, 0, unroll=4)
    student_rows_ref[...] = lanes_of_rows(parts_ref[...])


def store_copies(out_ref, line):
    out_ref[...] = jnp.broadcast_to(line[None], out_ref.shape)


def columns_body(sums_ref, exp_ref, *refs):
    *rider, scale_ref, rows_ref, parts_ref = refs
    scale = 1.0 / (jnp.sum(sums_ref[...], axis=0) * PROTOS)
    scale_ref[...] = scale
    step = 64

    def block(index, _):
        rows = pl.ds(pl.multiple_of(index * step, step), step)
        total = exp_ref[rows, :LANES] * scale[:, :LANES]
        for start in range(LANES, exp_ref.shape[1], LANES):
            total = total + exp_ref[rows, start : start + LANES] * scale[:, start : start + LANES]
        parts_ref[rows, :] = total
        return 0

    lax.fori_loop(0, exp_ref.shape[0] // step, block, 0, unroll=2)
    line = lanes_of_rows(parts_ref[...])
    peers, _, width = rows_ref.shape
    rows = line.shape[1]
    rows_ref[:, :, :rows] = jnp.broadcast_to(line[None], (peers, 1, rows))
    if rider:
        groups = rider[0].shape[1] // LANES
        for group in range(groups):
            lanes = rider[0][:, group * LANES : (group + 1) * LANES]
            some = slice(group * peers // groups, (group + 1) * peers // groups)
            rows_ref[some, :, rows:] = jnp.broadcast_to(lanes[None], (peers // groups, 1, LANES))


def rows_body(total_rows, sums_ref, exp_ref, cols_ref, *refs):
    *rider, scale_ref, parts_ref = refs
    sums = jnp.sum(sums_ref[...], axis=0)
    line = 1.0 / (sums[:, : exp_ref.shape[0]] * total_rows)
    if rider:
        rider[0][...] = sums[:, exp_ref.shape[0] :]
    scale_ref[...] = rows_on_sublanes(line)
    width = exp_ref.shape[1]
    parts_ref[...] = jnp.zeros_like(parts_ref)
    step = 64

    def block(index, _):
        rows = pl.ds(pl.multiple_of(index * step, step), step)
        scale = scale_ref[rows, :]
        for start in range(0, width, LANES):
            product = exp_ref[rows, start : start + LANES] * scale
            total = product[0:8]
            for r in range(8, step, 8):
                total = total + product[r : r + 8]
            parts_ref[:, start : start + LANES] += total
        return 0

    lax.fori_loop(0, exp_ref.shape[0] // step, block, 0, unroll=2)
    store_copies(cols_ref, jnp.sum(parts_ref[...], axis=0, keepdims=True))


def feature_body(
    total_rows,
    sums_ref, student_ref, cols_ref, teacher_exp_ref, student_exp_ref, unit_weight_ref, unit_ref, inverse_ref,
    mask_ref,
    placed_hbm, score_hbm, row_ref, total_ref, sum_ref, score_ref, placed_ref, sems,
):
    rows = teacher_exp_ref.shape[0]
    row_ref[...] = rows_on_sublanes(1.0 / (jnp.sum(sums_ref[...], axis=0) * total_rows))
    groups = rows // LANES
    step = student_ref.shape[0] // groups
    totals = jnp.concatenate([student_ref[group * step][:, rows:] for group in range(groups)], axis=1)
    total_ref[...] = rows_on_sublanes((1.0 / temp_student) / totals)

    protos = teacher_exp_ref.shape[1]
    halves = [slice(0, protos // 2), slice(protos // 2, protos)]
    stores = [
        pltpu.make_async_copy(score_ref.at[:, half], score_hbm.at[:, half], sems.at[index])
        for index, half in enumerate(halves)
    ]

    def score_of(half):
        for start in range(half.start, half.stop, TILE):
            cols = slice(start, start + TILE)
            target = teacher_exp_ref[:, cols] * spread(row_ref[...], TILE)
            target = target * (cols_ref[:, cols] * (total_rows / temp_student))
            score = (student_exp_ref[:, cols] * spread(total_ref[...], TILE) - target).astype(bf16)
            score_ref[:, cols] = score

    def product(half):
        return lax.dot_general(
            score_ref[:, half], unit_weight_ref[:, half], (((1,), (1,)), ((), ())), preferred_element_type=f32
        )

    score_of(halves[0])
    stores[0].start()
    sum_ref[...] = product(halves[0])
    score_of(halves[1])
    stores[1].start()
    sum_ref[...] += product(halves[1])
    images, masked = mask_ref.shape
    width = unit_ref.shape[1]
    shares = placed_ref.shape[0]
    share = placed_ref.shape[1] // images
    patch = lax.broadcasted_iota(jnp.int32, (shares * share, 2 * masked), 0)

    placed_stores = []
    for image in range(images):
        rows = slice(image * masked, (image + 1) * masked)
        unit = unit_ref[rows, :]
        total = sum_ref[rows, :]
        projection = jnp.sum(unit * total, axis=1, keepdims=True)
        gradient = (total - unit * projection) * spread(inverse_ref[rows, :], width)
        high = gradient.astype(bf16)
        low = (gradient - high.astype(f32)).astype(bf16)
        positions = mask_ref[image : image + 1, :]
        chosen = (patch == jnp.concatenate([positions, positions], axis=1)).astype(bf16)
        placed = jnp.dot(chosen, jnp.concatenate([high, low], axis=0), preferred_element_type=f32)
        where = pl.ds(image * share, share)
        placed_ref[:, where, :] = placed.reshape(shares, share, width)
        placed_stores.append(
            pltpu.make_async_copy(placed_ref.at[:, where], placed_hbm.at[:, where], sems.at[2 + image])
        )
        placed_stores[-1].start()
    for store in stores + placed_stores:
        store.wait()


def weight_body(
    score_hbm, weight_hbm, turned_ref, length_ref, mine_ref, other_ref, score_ref, weight_ref, sems
):
    levels, share = mine_ref.shape[:2]
    me = lax.axis_index("rows")
    core, level = me % 2, me // 2
    tiles = weight_ref.shape[1] // TILE
    weight_load = pltpu.make_async_copy(weight_hbm, weight_ref, sems.at[tiles])
    weight_load.start()
    loads = [
        pltpu.make_async_copy(
            score_hbm.at[:, pl.ds(tile * TILE, TILE)], score_ref.at[:, pl.ds(tile * TILE, TILE)], sems.at[tile]
        )
        for tile in range(tiles)
    ]
    for load in loads:
        load.start()
    weight_load.wait()
    for tile in range(tiles):
        cols = slice(tile * TILE, (tile + 1) * TILE)
        loads[tile].wait()
        total = jnp.dot(turned_ref[...], score_ref[:, cols], preferred_element_type=f32)
        inverse = 1.0 / length_ref[:, cols]
        unit = weight_ref[:, cols].astype(f32) * inverse
        dots = jnp.sum(unit * total, axis=0, keepdims=True)
        gradient = ((total - unit * dots) * inverse).reshape(levels, 2, share, TILE)
        for z in range(levels):
            place = pl.ds((z + levels - level) % levels, 1)
            mine_ref[place, :, cols] = jnp.where(core == 0, gradient[z, 0], gradient[z, 1])[None]
            other_ref[place, :, cols] = jnp.where(core == 0, gradient[z, 1], gradient[z, 0])[None]


def total_body(parts_ref, out_ref):
    out_ref[...] = jnp.sum(parts_ref[...], axis=0)


def everyones(copies, axis):
    return lax.all_to_all(copies, axis, 0, 0, tiled=True)


def send_rows(values, to):
    return lax.ppermute(values, "rows", [(i, to(i)) for i in range(lax.axis_size("rows"))])


def ring_share(parts, levels):
    def along(values, by):
        return send_rows(values, lambda i: (i + 2 * by) % (2 * levels))

    last = levels // 2
    total = parts[0]
    if levels > 1:
        up = parts[last]
        for k in range(last - 1, 0, -1):
            up = along(up, 1) + parts[k]
        total = total + along(up, 1)
    if levels > 2:
        down = parts[last + 1]
        for k in range(last + 2, levels):
            down = along(down, -1) + parts[k]
        total = total + along(down, -1)
    return total


def local(student_patches, teacher_patches, mask_index, student_weight, teacher_weight):
    images, patches, depth = student_patches.shape
    masked = mask_index.shape[1]
    rows = images * masked
    row_devices = lax.axis_size("rows")
    proto_devices = lax.axis_size("protos")
    total_rows = float(rows * row_devices)
    protos = student_weight.shape[1]
    work = 2 * rows * protos * depth

    teacher_exp, column_part, student_exp, student_part, unit, inverse, turned, unit_weight, length = call(
        first_body,
        [
            ((rows, protos), f32),
            ((row_devices, 1, protos), f32),
            ((rows, protos), f32),
            ((1, rows), f32),
            ((rows, depth), f32),
            ((rows, LANES), f32),
            ((depth, rows), bf16),
            ((depth, protos), bf16),
            ((1, protos), f32),
        ],
        (teacher_patches, teacher_weight, student_patches, student_weight, mask_index),
        [
            pltpu.VMEM(teacher_patches.shape, bf16),
            pltpu.VMEM(teacher_weight.shape, bf16),
            pltpu.VMEM(student_patches.shape, bf16),
            pltpu.VMEM(student_weight.shape, bf16),
            pltpu.VMEM(mask_index.shape, jnp.int32),
            pltpu.VMEM((rows, depth), bf16),
            pltpu.VMEM((rows, depth), bf16),
            pltpu.VMEM((rows, LANES), f32),
            pltpu.SemaphoreType.DMA((4 + images,)),
        ],
        limit=12, hbm=5, flops=2 * work, moved=2**23,
    )
    rider = student_part
    for sweep in range(SK_ITERS):
        column_sums = everyones(column_part, "rows")
        riders = [rider] if sweep < 2 else []
        col_scale, row_part = call(
            columns_body,
            [((1, protos), f32), ((proto_devices, 1, rows + LANES * len(riders)), f32)],
            (column_sums, teacher_exp, *riders),
            [pltpu.VMEM((rows, LANES), f32)],
            flops=2 * rows * protos, moved=2**23,
        )
        row_sums = everyones(row_part, "protos")
        if sweep == 1:
            student_sums = row_sums
        if sweep < SK_ITERS - 1:
            column_part, *riding = call(
                functools.partial(rows_body, total_rows),
                [((row_devices, 1, protos), f32)] + [((1, LANES), f32)] * (sweep == 0),
                (row_sums, teacher_exp),
                [pltpu.VMEM((rows, LANES), f32), pltpu.VMEM((8, protos), f32)],
                flops=2 * rows * protos, moved=2**23,
            )
            if sweep == 0:
                (rider,) = riding
    share = patches // proto_devices
    levels = row_devices // 2
    placed, score = call(
        functools.partial(feature_body, total_rows),
        [((proto_devices, images * share, depth), f32, pltpu.HBM), ((rows, protos), bf16, pltpu.HBM)],
        (row_sums, student_sums, col_scale, teacher_exp, student_exp, unit_weight, unit, inverse, mask_index),
        [
            pltpu.VMEM((rows, LANES), f32),
            pltpu.VMEM((rows, LANES), f32),
            pltpu.VMEM((rows, depth), f32),
            pltpu.VMEM((rows, protos), bf16),
            pltpu.VMEM((proto_devices, images * share, depth), f32),
            pltpu.SemaphoreType.DMA((2 + images,)),
        ],
        limit=16, flops=work, moved=2**24,
    )
    arrived = everyones(placed, "protos")
    mine, other = call(
        weight_body,
        [((levels, depth // row_devices, protos), f32)] * 2,
        (score, student_weight, turned, length),
        [
            pltpu.VMEM((rows, protos), bf16),
            pltpu.VMEM(student_weight.shape, bf16),
            pltpu.SemaphoreType.DMA((protos // TILE + 1,)),
        ],
        limit=12, hbm=2,
    )
    grad_weight = ring_share(mine + send_rows(other, lambda i: i ^ 1), levels)
    (grad_patches,) = call(
        total_body,
        [(arrived.shape[1:], f32, jax.ShapeDtypeStruct)],
        (arrived,),
    )
    return (grad_patches.reshape(images, share, depth), grad_weight)


def solution(mesh):
    placed = (
        P("rows", None, None),
        P("rows", None, None),
        P("rows", None),
        P(None, "protos"),
        P(None, "protos"),
    )
    return jax.shard_map(
        local,
        mesh=mesh,
        in_specs=placed,
        out_specs=(P("rows", "protos", None), P("rows", "protos")),
        check_vma=False,
    )
```

```python
import functools
import math

import jax
import jax.numpy as jnp
from jax import lax
from jax.experimental import pallas as pl
from jax.experimental.pallas import tpu as pltpu
from jax.sharding import PartitionSpec as P

PROTOS = 65536
SK_ITERS = 3
LANES = 128

epsilon = 1e-06
temp_student = 0.1
temp_teacher = 0.07

f32 = jnp.float32
bf16 = jnp.bfloat16


def call(body, outs, ins, scratch=(), limit=8, hbm=0, flops=0, moved=0):
    held = [pltpu.with_memory_space_constraint(array, pltpu.HBM) for array in ins[:hbm]]
    spaces = [pltpu.HBM] * hbm + [pltpu.VMEM] * (len(ins) - hbm)
    return pl.pallas_call(
        body,
        out_shape=[
            (space[0] if space else pltpu.VMEM)(shape, dtype) for shape, dtype, *space in outs
        ],
        in_specs=[pl.BlockSpec(memory_space=space) for space in spaces],
        out_specs=[
            pl.BlockSpec(memory_space=pltpu.HBM if space and space[0] is pltpu.HBM else pltpu.VMEM)
            for _, _, *space in outs
        ],
        scratch_shapes=list(scratch),
        compiler_params=pltpu.CompilerParams(vmem_limit_bytes=limit * 2**20),
        cost_estimate=pl.CostEstimate(flops=flops, bytes_accessed=moved, transcendentals=0),
    )(*held, *ins[hbm:])


def pick(patches_ref, positions, image):
    patches = patches_ref.shape[1]
    masked = positions.shape[0]
    column = lax.broadcasted_iota(jnp.int32, (masked, patches), 1).astype(f32)
    chosen = (column == positions[:, image : image + 1]).astype(bf16)
    return jnp.dot(chosen, patches_ref[image], preferred_element_type=f32)


def lanes_of_rows(parts):
    groups = parts.shape[0] // LANES
    lane = lax.broadcasted_iota(jnp.int32, (LANES, LANES), 1)
    table = jnp.zeros((LANES, LANES), f32)
    for group in range(groups):
        column = jnp.sum(parts[group * LANES : (group + 1) * LANES], axis=1, keepdims=True)
        table = jnp.where(lane == group, column, table)
    table = table.T
    return jnp.concatenate([table[group : group + 1] for group in range(groups)], axis=1)


def fold_lanes(values):
    total = values[:, :LANES]
    for start in range(LANES, values.shape[1], LANES):
        total = total + values[:, start : start + LANES]
    return total


def rows_on_sublanes(line):
    pieces = [
        jnp.broadcast_to(line[:, s : s + LANES], (LANES, LANES)).T
        for s in range(0, line.shape[1], LANES)
    ]
    return jnp.concatenate(pieces, axis=0)


def spread(column, width):
    return jnp.concatenate([column] * (width // LANES), axis=1)


def unit_columns(weight_ref, cols):
    weight = weight_ref[:, cols].astype(f32)
    length = jnp.sqrt(jnp.sum(weight * weight, axis=0, keepdims=True) + epsilon)
    return weight * (1.0 / length), length


TILE = 256
LOG2_E = math.log2(math.e)


def first_body(
    teacher_hbm, teacher_weight_hbm, student_hbm, student_weight_hbm, mask_hbm,
    teacher_exp_ref, cols_ref, student_exp_ref, student_rows_ref, unit_ref, inverse_ref, turned_ref, unit_weight_ref,
    length_ref,
    teacher_ref, teacher_weight_ref, student_ref, student_weight_ref, mask_ref, teacher_bf_ref, student_bf_ref, parts_ref, sems,
):
    images, masked = mask_ref.shape
    protos = teacher_exp_ref.shape[1]
    loads = [
        pltpu.make_async_copy(source, target, sems.at[index])
        for index, (source, target) in enumerate(
            (
                (mask_hbm, mask_ref),
                (teacher_hbm, teacher_ref),
                (teacher_weight_hbm, teacher_weight_ref),
                (student_hbm, student_ref),
                (student_weight_hbm, student_weight_ref),
            )
        )
    ]
    for load in loads:
        load.start()
    loads[0].wait()
    positions = mask_ref[...].astype(f32).T
    loads[1].wait()
    for image in range(images):
        picked = pick(teacher_ref, positions, image)
        length = jnp.sqrt(jnp.sum(picked * picked, axis=1, keepdims=True) + epsilon)
        rows = slice(image * masked, (image + 1) * masked)
        teacher_bf_ref[rows, :] = (picked * (1.0 / length)).astype(bf16)
    loads[2].wait()

    def teacher_tile(tile, _):
        cols = pl.ds(pl.multiple_of(tile * TILE, TILE), TILE)
        unit = unit_columns(teacher_weight_ref, cols)[0].astype(bf16)
        products = jnp.dot(teacher_bf_ref[...], unit, preferred_element_type=f32)
        exps = jnp.exp2(products * (LOG2_E / temp_teacher))
        teacher_exp_ref[:, cols] = exps
        line = jnp.sum(exps, axis=0, keepdims=True)
        cols_ref[:, :, cols] = jnp.broadcast_to(line[None], (cols_ref.shape[0], 1, TILE))
        return 0

    lax.fori_loop(0, protos // TILE, teacher_tile, 0, unroll=4)
    loads[3].wait()

    for image in range(images):
        picked = pick(student_ref, positions, image)
        inverse = 1.0 / jnp.sqrt(jnp.sum(picked * picked, axis=1, keepdims=True) + epsilon)
        unit = picked * inverse
        rows = slice(image * masked, (image + 1) * masked)
        unit_ref[rows, :] = unit
        student_bf_ref[rows, :] = unit.astype(bf16)
        turned_ref[:, rows] = unit.T.astype(bf16)
        inverse_ref[rows, :] = jnp.broadcast_to(inverse, (masked, LANES))
    parts_ref[...] = jnp.zeros_like(parts_ref)
    loads[4].wait()

    def student_tile(tile, _):
        cols = pl.ds(pl.multiple_of(tile * TILE, TILE), TILE)
        unit, length = unit_columns(student_weight_ref, cols)
        length_ref[:, cols] = length
        unit = unit.astype(bf16)
        unit_weight_ref[:, cols] = unit
        products = jnp.dot(student_bf_ref[...], unit, preferred_element_type=f32)
        exps = jnp.exp2(products * (LOG2_E / temp_student))
        student_exp_ref[:, cols] = exps
        parts_ref[...] += fold_lanes(exps)
        return 0

    lax.fori_loop(0, protos // TILE, student_tile, 0, unroll=4)
    student_rows_ref[...] = lanes_of_rows(parts_ref[...])


def store_copies(out_ref, line):
    out_ref[...] = jnp.broadcast_to(line[None], out_ref.shape)


def columns_body(sums_ref, exp_ref, *refs):
    *rider, scale_ref, rows_ref, parts_ref = refs
    scale = 1.0 / (jnp.sum(sums_ref[...], axis=0) * PROTOS)
    scale_ref[...] = scale
    step = 64

    def block(index, _):
        rows = pl.ds(pl.multiple_of(index * step, step), step)
        total = exp_ref[rows, :LANES] * scale[:, :LANES]
        for start in range(LANES, exp_ref.shape[1], LANES):
            total = total + exp_ref[rows, start : start + LANES] * scale[:, start : start + LANES]
        parts_ref[rows, :] = total
        return 0

    lax.fori_loop(0, exp_ref.shape[0] // step, block, 0, unroll=2)
    line = lanes_of_rows(parts_ref[...])
    peers, _, width = rows_ref.shape
    rows = line.shape[1]
    rows_ref[:, :, :rows] = jnp.broadcast_to(line[None], (peers, 1, rows))
    if rider:
        groups = rider[0].shape[1] // LANES
        for group in range(groups):
            lanes = rider[0][:, group * LANES : (group + 1) * LANES]
            some = slice(group * peers // groups, (group + 1) * peers // groups)
            rows_ref[some, :, rows:] = jnp.broadcast_to(lanes[None], (peers // groups, 1, LANES))


def rows_body(total_rows, sums_ref, exp_ref, cols_ref, *refs):
    *rider, scale_ref, parts_ref = refs
    sums = jnp.sum(sums_ref[...], axis=0)
    line = 1.0 / (sums[:, : exp_ref.shape[0]] * total_rows)
    if rider:
        rider[0][...] = sums[:, exp_ref.shape[0] :]
    scale_ref[...] = rows_on_sublanes(line)
    width = exp_ref.shape[1]
    parts_ref[...] = jnp.zeros_like(parts_ref)
    step = 64

    def block(index, _):
        rows = pl.ds(pl.multiple_of(index * step, step), step)
        scale = scale_ref[rows, :]
        for start in range(0, width, LANES):
            product = exp_ref[rows, start : start + LANES] * scale
            total = product[0:8]
            for r in range(8, step, 8):
                total = total + product[r : r + 8]
            parts_ref[:, start : start + LANES] += total
        return 0

    lax.fori_loop(0, exp_ref.shape[0] // step, block, 0, unroll=2)
    store_copies(cols_ref, jnp.sum(parts_ref[...], axis=0, keepdims=True))


def feature_body(
    total_rows,
    sums_ref, student_ref, cols_ref, teacher_exp_ref, student_exp_ref, unit_weight_ref, unit_ref, inverse_ref,
    mask_ref,
    placed_hbm, score_hbm, row_ref, total_ref, sum_ref, score_ref, placed_ref, sems,
):
    rows = teacher_exp_ref.shape[0]
    row_ref[...] = rows_on_sublanes(1.0 / (jnp.sum(sums_ref[...], axis=0) * total_rows))
    groups = rows // LANES
    step = student_ref.shape[0] // groups
    totals = jnp.concatenate([student_ref[group * step][:, rows:] for group in range(groups)], axis=1)
    total_ref[...] = rows_on_sublanes((1.0 / temp_student) / totals)

    protos = teacher_exp_ref.shape[1]
    halves = [slice(0, protos // 2), slice(protos // 2, protos)]
    stores = [
        pltpu.make_async_copy(score_ref.at[:, half], score_hbm.at[:, half], sems.at[index])
        for index, half in enumerate(halves)
    ]

    def score_of(half):
        for start in range(half.start, half.stop, TILE):
            cols = slice(start, start + TILE)
            target = teacher_exp_ref[:, cols] * spread(row_ref[...], TILE)
            target = target * (cols_ref[:, cols] * (total_rows / temp_student))
            score = (student_exp_ref[:, cols] * spread(total_ref[...], TILE) - target).astype(bf16)
            score_ref[:, cols] = score

    def product(half):
        return lax.dot_general(
            score_ref[:, half], unit_weight_ref[:, half], (((1,), (1,)), ((), ())), preferred_element_type=f32
        )

    score_of(halves[0])
    stores[0].start()
    sum_ref[...] = product(halves[0])
    score_of(halves[1])
    stores[1].start()
    sum_ref[...] += product(halves[1])
    images, masked = mask_ref.shape
    width = unit_ref.shape[1]
    shares = placed_ref.shape[0]
    share = placed_ref.shape[1] // images
    patch = lax.broadcasted_iota(jnp.int32, (shares * share, 2 * masked), 0)

    placed_stores = []
    for image in range(images):
        rows = slice(image * masked, (image + 1) * masked)
        unit = unit_ref[rows, :]
        total = sum_ref[rows, :]
        projection = jnp.sum(unit * total, axis=1, keepdims=True)
        gradient = (total - unit * projection) * spread(inverse_ref[rows, :], width)
        high = gradient.astype(bf16)
        low = (gradient - high.astype(f32)).astype(bf16)
        positions = mask_ref[image : image + 1, :]
        chosen = (patch == jnp.concatenate([positions, positions], axis=1)).astype(bf16)
        placed = jnp.dot(chosen, jnp.concatenate([high, low], axis=0), preferred_element_type=f32)
        where = pl.ds(image * share, share)
        placed_ref[:, where, :] = placed.reshape(shares, share, width)
        placed_stores.append(
            pltpu.make_async_copy(placed_ref.at[:, where], placed_hbm.at[:, where], sems.at[2 + image])
        )
        placed_stores[-1].start()
    for store in stores + placed_stores:
        store.wait()


def weight_body(
    score_hbm, weight_hbm, turned_ref, length_ref, mine_ref, other_ref, score_ref, weight_ref, sems
):
    levels, share = mine_ref.shape[:2]
    me = lax.axis_index("rows")
    core, level = me % 2, me // 2
    protos = weight_ref.shape[1]
    half = protos // 2
    weight_load = pltpu.make_async_copy(weight_hbm, weight_ref, sems.at[2])
    loads = [
        pltpu.make_async_copy(
            score_hbm.at[:, pl.ds(start, half)], score_ref.at[:, pl.ds(start, half)], sems.at[index]
        )
        for index, start in enumerate((0, half))
    ]
    for load in (loads[0], weight_load, loads[1]):
        load.start()
    weight_load.wait()
    for start in range(0, protos, TILE):
        cols = slice(start, start + TILE)
        if start % half == 0:
            loads[start // half].wait()
        total = jnp.dot(turned_ref[...], score_ref[:, cols], preferred_element_type=f32)
        inverse = 1.0 / length_ref[:, cols]
        unit = weight_ref[:, cols].astype(f32) * inverse
        dots = jnp.sum(unit * total, axis=0, keepdims=True)
        gradient = ((total - unit * dots) * inverse).reshape(levels, 2, share, TILE)
        for z in range(levels):
            place = pl.ds((z + levels - level) % levels, 1)
            mine_ref[place, :, cols] = jnp.where(core == 0, gradient[z, 0], gradient[z, 1])[None]
            other_ref[place, :, cols] = jnp.where(core == 0, gradient[z, 1], gradient[z, 0])[None]


def total_body(parts_ref, out_ref):
    out_ref[...] = jnp.sum(parts_ref[...], axis=0)


def everyones(copies, axis):
    return lax.all_to_all(copies, axis, 0, 0, tiled=True)


def send_rows(values, to):
    return lax.ppermute(values, "rows", [(i, to(i)) for i in range(lax.axis_size("rows"))])


def ring_share(parts, levels):
    def along(values, by):
        return send_rows(values, lambda i: (i + 2 * by) % (2 * levels))

    last = levels // 2
    total = parts[0]
    if levels > 1:
        up = parts[last]
        for k in range(last - 1, 0, -1):
            up = along(up, 1) + parts[k]
        total = total + along(up, 1)
    if levels > 2:
        down = parts[last + 1]
        for k in range(last + 2, levels):
            down = along(down, -1) + parts[k]
        total = total + along(down, -1)
    return total


def local(student_patches, teacher_patches, mask_index, student_weight, teacher_weight):
    images, patches, depth = student_patches.shape
    masked = mask_index.shape[1]
    rows = images * masked
    row_devices = lax.axis_size("rows")
    proto_devices = lax.axis_size("protos")
    total_rows = float(rows * row_devices)
    protos = student_weight.shape[1]
    work = 2 * rows * protos * depth

    teacher_exp, column_part, student_exp, student_part, unit, inverse, turned, unit_weight, length = call(
        first_body,
        [
            ((rows, protos), f32),
            ((row_devices, 1, protos), f32),
            ((rows, protos), f32),
            ((1, rows), f32),
            ((rows, depth), f32),
            ((rows, LANES), f32),
            ((depth, rows), bf16),
            ((depth, protos), bf16),
            ((1, protos), f32),
        ],
        (teacher_patches, teacher_weight, student_patches, student_weight, mask_index),
        [
            pltpu.VMEM(teacher_patches.shape, bf16),
            pltpu.VMEM(teacher_weight.shape, bf16),
            pltpu.VMEM(student_patches.shape, bf16),
            pltpu.VMEM(student_weight.shape, bf16),
            pltpu.VMEM(mask_index.shape, jnp.int32),
            pltpu.VMEM((rows, depth), bf16),
            pltpu.VMEM((rows, depth), bf16),
            pltpu.VMEM((rows, LANES), f32),
            pltpu.SemaphoreType.DMA((5,)),
        ],
        limit=12, hbm=5, flops=2 * work, moved=2**23,
    )
    rider = student_part
    for sweep in range(SK_ITERS):
        column_sums = everyones(column_part, "rows")
        riders = [rider] if sweep < 2 else []
        col_scale, row_part = call(
            columns_body,
            [((1, protos), f32), ((proto_devices, 1, rows + LANES * len(riders)), f32)],
            (column_sums, teacher_exp, *riders),
            [pltpu.VMEM((rows, LANES), f32)],
            flops=2 * rows * protos, moved=2**23,
        )
        row_sums = everyones(row_part, "protos")
        if sweep == 1:
            student_sums = row_sums
        if sweep < SK_ITERS - 1:
            column_part, *riding = call(
                functools.partial(rows_body, total_rows),
                [((row_devices, 1, protos), f32)] + [((1, LANES), f32)] * (sweep == 0),
                (row_sums, teacher_exp),
                [pltpu.VMEM((rows, LANES), f32), pltpu.VMEM((8, protos), f32)],
                flops=2 * rows * protos, moved=2**23,
            )
            if sweep == 0:
                (rider,) = riding
    share = patches // proto_devices
    levels = row_devices // 2
    placed, score = call(
        functools.partial(feature_body, total_rows),
        [((proto_devices, images * share, depth), f32, pltpu.HBM), ((rows, protos), bf16, pltpu.HBM)],
        (row_sums, student_sums, col_scale, teacher_exp, student_exp, unit_weight, unit, inverse, mask_index),
        [
            pltpu.VMEM((rows, LANES), f32),
            pltpu.VMEM((rows, LANES), f32),
            pltpu.VMEM((rows, depth), f32),
            pltpu.VMEM((rows, protos), bf16),
            pltpu.VMEM((proto_devices, images * share, depth), f32),
            pltpu.SemaphoreType.DMA((2 + images,)),
        ],
        limit=16, flops=work, moved=2**24,
    )
    arrived = everyones(placed, "protos")
    mine, other = call(
        weight_body,
        [((levels, depth // row_devices, protos), f32)] * 2,
        (score, student_weight, turned, length),
        [
            pltpu.VMEM((rows, protos), bf16),
            pltpu.VMEM(student_weight.shape, bf16),
            pltpu.SemaphoreType.DMA((3,)),
        ],
        limit=12, hbm=2,
    )
    grad_weight = ring_share(mine + send_rows(other, lambda i: i ^ 1), levels)
    (grad_patches,) = call(
        total_body,
        [(arrived.shape[1:], f32, jax.ShapeDtypeStruct)],
        (arrived,),
    )
    return (grad_patches.reshape(images, share, depth), grad_weight)


def solution(mesh):
    placed = (
        P("rows", None, None),
        P("rows", None, None),
        P("rows", None),
        P(None, "protos"),
        P(None, "protos"),
    )
    return jax.shard_map(
        local,
        mesh=mesh,
        in_specs=placed,
        out_specs=(P("rows", "protos", None), P("rows", "protos")),
        check_vma=False,
    )
```

```python
import functools
import math

import jax
import jax.numpy as jnp
from jax import lax
from jax.experimental import pallas as pl
from jax.experimental.pallas import tpu as pltpu
from jax.sharding import PartitionSpec as P

PROTOS = 65536
SK_ITERS = 3
LANES = 128

epsilon = 1e-06
temp_student = 0.1
temp_teacher = 0.07

f32 = jnp.float32
bf16 = jnp.bfloat16


def call(body, outs, ins, scratch=(), limit=8, hbm=0, flops=0, moved=0):
    held = [pltpu.with_memory_space_constraint(array, pltpu.HBM) for array in ins[:hbm]]
    spaces = [pltpu.HBM] * hbm + [pltpu.VMEM] * (len(ins) - hbm)
    return pl.pallas_call(
        body,
        out_shape=[
            (space[0] if space else pltpu.VMEM)(shape, dtype) for shape, dtype, *space in outs
        ],
        in_specs=[pl.BlockSpec(memory_space=space) for space in spaces],
        out_specs=[
            pl.BlockSpec(memory_space=pltpu.HBM if space and space[0] is pltpu.HBM else pltpu.VMEM)
            for _, _, *space in outs
        ],
        scratch_shapes=list(scratch),
        compiler_params=pltpu.CompilerParams(vmem_limit_bytes=limit * 2**20),
        cost_estimate=pl.CostEstimate(flops=flops, bytes_accessed=moved, transcendentals=0),
    )(*held, *ins[hbm:])


def pick(patches_ref, positions, image):
    patches = patches_ref.shape[1]
    masked = positions.shape[0]
    column = lax.broadcasted_iota(jnp.int32, (masked, patches), 1).astype(f32)
    chosen = (column == positions[:, image : image + 1]).astype(bf16)
    return jnp.dot(chosen, patches_ref[image], preferred_element_type=f32)


def lanes_of_rows(parts):
    groups = parts.shape[0] // LANES
    lane = lax.broadcasted_iota(jnp.int32, (LANES, LANES), 1)
    table = jnp.zeros((LANES, LANES), f32)
    for group in range(groups):
        column = jnp.sum(parts[group * LANES : (group + 1) * LANES], axis=1, keepdims=True)
        table = jnp.where(lane == group, column, table)
    table = table.T
    return jnp.concatenate([table[group : group + 1] for group in range(groups)], axis=1)


def fold_lanes(values):
    total = values[:, :LANES]
    for start in range(LANES, values.shape[1], LANES):
        total = total + values[:, start : start + LANES]
    return total


def rows_on_sublanes(line):
    pieces = [
        jnp.broadcast_to(line[:, s : s + LANES], (LANES, LANES)).T
        for s in range(0, line.shape[1], LANES)
    ]
    return jnp.concatenate(pieces, axis=0)


def spread(column, width):
    return jnp.concatenate([column] * (width // LANES), axis=1)


def unit_columns(weight_ref, cols):
    weight = weight_ref[:, cols].astype(f32)
    length = jnp.sqrt(jnp.sum(weight * weight, axis=0, keepdims=True) + epsilon)
    return weight * (1.0 / length), length


TILE = 256
LOG2_E = math.log2(math.e)


def first_body(
    teacher_hbm, teacher_weight_hbm, student_hbm, student_weight_hbm, mask_hbm,
    teacher_exp_ref, cols_ref, student_exp_ref, student_rows_ref, unit_ref, inverse_ref, turned_ref, unit_weight_ref,
    length_ref,
    teacher_ref, teacher_weight_ref, student_ref, student_weight_ref, mask_ref, teacher_bf_ref, student_bf_ref, parts_ref, sems,
):
    images, masked = mask_ref.shape
    protos = teacher_exp_ref.shape[1]
    loads = [
        pltpu.make_async_copy(source, target, sems.at[index])
        for index, (source, target) in enumerate(
            (
                (mask_hbm, mask_ref),
                (teacher_hbm, teacher_ref),
                (teacher_weight_hbm, teacher_weight_ref),
                (student_hbm, student_ref),
                (student_weight_hbm, student_weight_ref),
            )
        )
    ]
    for load in loads:
        load.start()
    loads[0].wait()
    positions = mask_ref[...].astype(f32).T
    loads[1].wait()
    for image in range(images):
        picked = pick(teacher_ref, positions, image)
        length = jnp.sqrt(jnp.sum(picked * picked, axis=1, keepdims=True) + epsilon)
        rows = slice(image * masked, (image + 1) * masked)
        teacher_bf_ref[rows, :] = (picked * (1.0 / length)).astype(bf16)
    loads[2].wait()

    def teacher_tile(tile, _):
        cols = pl.ds(pl.multiple_of(tile * TILE, TILE), TILE)
        unit = unit_columns(teacher_weight_ref, cols)[0].astype(bf16)
        products = jnp.dot(teacher_bf_ref[...], unit, preferred_element_type=f32)
        exps = jnp.exp2(products * (LOG2_E / temp_teacher))
        teacher_exp_ref[:, cols] = exps
        line = jnp.sum(exps, axis=0, keepdims=True)
        cols_ref[:, :, cols] = jnp.broadcast_to(line[None], (cols_ref.shape[0], 1, TILE))
        return 0

    lax.fori_loop(0, protos // TILE, teacher_tile, 0, unroll=8)
    loads[3].wait()

    for image in range(images):
        picked = pick(student_ref, positions, image)
        inverse = 1.0 / jnp.sqrt(jnp.sum(picked * picked, axis=1, keepdims=True) + epsilon)
        unit = picked * inverse
        rows = slice(image * masked, (image + 1) * masked)
        unit_ref[rows, :] = unit
        student_bf_ref[rows, :] = unit.astype(bf16)
        turned_ref[:, rows] = unit.T.astype(bf16)
        inverse_ref[rows, :] = jnp.broadcast_to(inverse, (masked, LANES))
    parts_ref[...] = jnp.zeros_like(parts_ref)
    loads[4].wait()

    def student_tile(tile, _):
        cols = pl.ds(pl.multiple_of(tile * TILE, TILE), TILE)
        unit, length = unit_columns(student_weight_ref, cols)
        length_ref[:, cols] = length
        unit = unit.astype(bf16)
        unit_weight_ref[:, cols] = unit
        products = jnp.dot(student_bf_ref[...], unit, preferred_element_type=f32)
        exps = jnp.exp2(products * (LOG2_E / temp_student))
        student_exp_ref[:, cols] = exps
        parts_ref[...] += fold_lanes(exps)
        return 0

    lax.fori_loop(0, protos // TILE, student_tile, 0, unroll=8)
    student_rows_ref[...] = lanes_of_rows(parts_ref[...])


def store_copies(out_ref, line):
    out_ref[...] = jnp.broadcast_to(line[None], out_ref.shape)


def columns_body(sums_ref, exp_ref, *refs):
    *rider, scale_ref, rows_ref, parts_ref = refs
    scale = 1.0 / (jnp.sum(sums_ref[...], axis=0) * PROTOS)
    scale_ref[...] = scale
    step = 64

    def block(index, _):
        rows = pl.ds(pl.multiple_of(index * step, step), step)
        total = exp_ref[rows, :LANES] * scale[:, :LANES]
        for start in range(LANES, exp_ref.shape[1], LANES):
            total = total + exp_ref[rows, start : start + LANES] * scale[:, start : start + LANES]
        parts_ref[rows, :] = total
        return 0

    lax.fori_loop(0, exp_ref.shape[0] // step, block, 0, unroll=4)
    line = lanes_of_rows(parts_ref[...])
    peers, _, width = rows_ref.shape
    rows = line.shape[1]
    rows_ref[:, :, :rows] = jnp.broadcast_to(line[None], (peers, 1, rows))
    if rider:
        groups = rider[0].shape[1] // LANES
        for group in range(groups):
            lanes = rider[0][:, group * LANES : (group + 1) * LANES]
            some = slice(group * peers // groups, (group + 1) * peers // groups)
            rows_ref[some, :, rows:] = jnp.broadcast_to(lanes[None], (peers // groups, 1, LANES))


def rows_body(total_rows, sums_ref, exp_ref, cols_ref, *refs):
    *rider, scale_ref, parts_ref = refs
    sums = jnp.sum(sums_ref[...], axis=0)
    line = 1.0 / (sums[:, : exp_ref.shape[0]] * total_rows)
    if rider:
        rider[0][...] = sums[:, exp_ref.shape[0] :]
    scale_ref[...] = rows_on_sublanes(line)
    width = exp_ref.shape[1]
    parts_ref[...] = jnp.zeros_like(parts_ref)
    step = 64

    def block(index, _):
        rows = pl.ds(pl.multiple_of(index * step, step), step)
        scale = scale_ref[rows, :]
        for start in range(0, width, LANES):
            product = exp_ref[rows, start : start + LANES] * scale
            total = product[0:8]
            for r in range(8, step, 8):
                total = total + product[r : r + 8]
            parts_ref[:, start : start + LANES] += total
        return 0

    lax.fori_loop(0, exp_ref.shape[0] // step, block, 0, unroll=4)
    store_copies(cols_ref, jnp.sum(parts_ref[...], axis=0, keepdims=True))


def feature_body(
    total_rows,
    sums_ref, student_ref, cols_ref, teacher_exp_ref, student_exp_ref, unit_weight_ref, unit_ref, inverse_ref,
    mask_ref,
    placed_hbm, score_hbm, row_ref, total_ref, sum_ref, score_ref, placed_ref, sems,
):
    rows = teacher_exp_ref.shape[0]
    row_ref[...] = rows_on_sublanes(1.0 / (jnp.sum(sums_ref[...], axis=0) * total_rows))
    groups = rows // LANES
    step = student_ref.shape[0] // groups
    totals = jnp.concatenate([student_ref[group * step][:, rows:] for group in range(groups)], axis=1)
    total_ref[...] = rows_on_sublanes((1.0 / temp_student) / totals)

    protos = teacher_exp_ref.shape[1]
    halves = [slice(0, protos // 2), slice(protos // 2, protos)]
    stores = [
        pltpu.make_async_copy(score_ref.at[:, half], score_hbm.at[:, half], sems.at[index])
        for index, half in enumerate(halves)
    ]

    def score_of(half):
        for start in range(half.start, half.stop, TILE):
            cols = slice(start, start + TILE)
            target = teacher_exp_ref[:, cols] * spread(row_ref[...], TILE)
            target = target * (cols_ref[:, cols] * (total_rows / temp_student))
            score = (student_exp_ref[:, cols] * spread(total_ref[...], TILE) - target).astype(bf16)
            score_ref[:, cols] = score

    def product(half):
        return lax.dot_general(
            score_ref[:, half], unit_weight_ref[:, half], (((1,), (1,)), ((), ())), preferred_element_type=f32
        )

    score_of(halves[0])
    stores[0].start()
    sum_ref[...] = product(halves[0])
    score_of(halves[1])
    stores[1].start()
    sum_ref[...] += product(halves[1])
    images, masked = mask_ref.shape
    width = unit_ref.shape[1]
    shares = placed_ref.shape[0]
    share = placed_ref.shape[1] // images
    patch = lax.broadcasted_iota(jnp.int32, (shares * share, 2 * masked), 0)

    placed_stores = []
    for image in range(images):
        rows = slice(image * masked, (image + 1) * masked)
        unit = unit_ref[rows, :]
        total = sum_ref[rows, :]
        projection = jnp.sum(unit * total, axis=1, keepdims=True)
        gradient = (total - unit * projection) * spread(inverse_ref[rows, :], width)
        high = gradient.astype(bf16)
        low = (gradient - high.astype(f32)).astype(bf16)
        positions = mask_ref[image : image + 1, :]
        chosen = (patch == jnp.concatenate([positions, positions], axis=1)).astype(bf16)
        placed = jnp.dot(chosen, jnp.concatenate([high, low], axis=0), preferred_element_type=f32)
        where = pl.ds(image * share, share)
        placed_ref[:, where, :] = placed.reshape(shares, share, width)
        placed_stores.append(
            pltpu.make_async_copy(placed_ref.at[:, where], placed_hbm.at[:, where], sems.at[2 + image])
        )
        placed_stores[-1].start()
    for store in stores + placed_stores:
        store.wait()


def weight_body(
    score_hbm, weight_hbm, turned_ref, length_ref, mine_ref, other_ref, score_ref, weight_ref, sems
):
    levels, share = mine_ref.shape[:2]
    me = lax.axis_index("rows")
    core, level = me % 2, me // 2
    protos = weight_ref.shape[1]
    half = protos // 2
    weight_load = pltpu.make_async_copy(weight_hbm, weight_ref, sems.at[2])
    loads = [
        pltpu.make_async_copy(
            score_hbm.at[:, pl.ds(start, half)], score_ref.at[:, pl.ds(start, half)], sems.at[index]
        )
        for index, start in enumerate((0, half))
    ]
    for load in (loads[0], weight_load, loads[1]):
        load.start()
    weight_load.wait()
    for start in range(0, protos, TILE):
        cols = slice(start, start + TILE)
        if start % half == 0:
            loads[start // half].wait()
        total = jnp.dot(turned_ref[...], score_ref[:, cols], preferred_element_type=f32)
        inverse = 1.0 / length_ref[:, cols]
        unit = weight_ref[:, cols].astype(f32) * inverse
        dots = jnp.sum(unit * total, axis=0, keepdims=True)
        gradient = ((total - unit * dots) * inverse).reshape(levels, 2, share, TILE)
        for z in range(levels):
            place = pl.ds((z + levels - level) % levels, 1)
            mine_ref[place, :, cols] = jnp.where(core == 0, gradient[z, 0], gradient[z, 1])[None]
            other_ref[place, :, cols] = jnp.where(core == 0, gradient[z, 1], gradient[z, 0])[None]


def total_body(parts_ref, out_ref):
    out_ref[...] = jnp.sum(parts_ref[...], axis=0)


def everyones(copies, axis):
    return lax.all_to_all(copies, axis, 0, 0, tiled=True)


def send_rows(values, to):
    return lax.ppermute(values, "rows", [(i, to(i)) for i in range(lax.axis_size("rows"))])


def ring_share(parts, levels):
    def along(values, by):
        return send_rows(values, lambda i: (i + 2 * by) % (2 * levels))

    last = levels // 2
    total = parts[0]
    if levels > 1:
        up = parts[last]
        for k in range(last - 1, 0, -1):
            up = along(up, 1) + parts[k]
        total = total + along(up, 1)
    if levels > 2:
        down = parts[last + 1]
        for k in range(last + 2, levels):
            down = along(down, -1) + parts[k]
        total = total + along(down, -1)
    return total


def local(student_patches, teacher_patches, mask_index, student_weight, teacher_weight):
    images, patches, depth = student_patches.shape
    masked = mask_index.shape[1]
    rows = images * masked
    row_devices = lax.axis_size("rows")
    proto_devices = lax.axis_size("protos")
    total_rows = float(rows * row_devices)
    protos = student_weight.shape[1]
    work = 2 * rows * protos * depth

    teacher_exp, column_part, student_exp, student_part, unit, inverse, turned, unit_weight, length = call(
        first_body,
        [
            ((rows, protos), f32),
            ((row_devices, 1, protos), f32),
            ((rows, protos), f32),
            ((1, rows), f32),
            ((rows, depth), f32),
            ((rows, LANES), f32),
            ((depth, rows), bf16),
            ((depth, protos), bf16),
            ((1, protos), f32),
        ],
        (teacher_patches, teacher_weight, student_patches, student_weight, mask_index),
        [
            pltpu.VMEM(teacher_patches.shape, bf16),
            pltpu.VMEM(teacher_weight.shape, bf16),
            pltpu.VMEM(student_patches.shape, bf16),
            pltpu.VMEM(student_weight.shape, bf16),
            pltpu.VMEM(mask_index.shape, jnp.int32),
            pltpu.VMEM((rows, depth), bf16),
            pltpu.VMEM((rows, depth), bf16),
            pltpu.VMEM((rows, LANES), f32),
            pltpu.SemaphoreType.DMA((5,)),
        ],
        limit=12, hbm=5, flops=2 * work, moved=2**23,
    )
    rider = student_part
    for sweep in range(SK_ITERS):
        column_sums = everyones(column_part, "rows")
        riders = [rider] if sweep < 2 else []
        col_scale, row_part = call(
            columns_body,
            [((1, protos), f32), ((proto_devices, 1, rows + LANES * len(riders)), f32)],
            (column_sums, teacher_exp, *riders),
            [pltpu.VMEM((rows, LANES), f32)],
            flops=2 * rows * protos, moved=2**23,
        )
        row_sums = everyones(row_part, "protos")
        if sweep == 1:
            student_sums = row_sums
        if sweep < SK_ITERS - 1:
            column_part, *riding = call(
                functools.partial(rows_body, total_rows),
                [((row_devices, 1, protos), f32)] + [((1, LANES), f32)] * (sweep == 0),
                (row_sums, teacher_exp),
                [pltpu.VMEM((rows, LANES), f32), pltpu.VMEM((8, protos), f32)],
                flops=2 * rows * protos, moved=2**23,
            )
            if sweep == 0:
                (rider,) = riding
    share = patches // proto_devices
    levels = row_devices // 2
    placed, score = call(
        functools.partial(feature_body, total_rows),
        [((proto_devices, images * share, depth), f32, pltpu.HBM), ((rows, protos), bf16, pltpu.HBM)],
        (row_sums, student_sums, col_scale, teacher_exp, student_exp, unit_weight, unit, inverse, mask_index),
        [
            pltpu.VMEM((rows, LANES), f32),
            pltpu.VMEM((rows, LANES), f32),
            pltpu.VMEM((rows, depth), f32),
            pltpu.VMEM((rows, protos), bf16),
            pltpu.VMEM((proto_devices, images * share, depth), f32),
            pltpu.SemaphoreType.DMA((2 + images,)),
        ],
        limit=16, flops=work, moved=2**24,
    )
    arrived = everyones(placed, "protos")
    mine, other = call(
        weight_body,
        [((levels, depth // row_devices, protos), f32)] * 2,
        (score, student_weight, turned, length),
        [
            pltpu.VMEM((rows, protos), bf16),
            pltpu.VMEM(student_weight.shape, bf16),
            pltpu.SemaphoreType.DMA((3,)),
        ],
        limit=12, hbm=2,
    )
    grad_weight = ring_share(mine + send_rows(other, lambda i: i ^ 1), levels)
    (grad_patches,) = call(
        total_body,
        [(arrived.shape[1:], f32, jax.ShapeDtypeStruct)],
        (arrived,),
    )
    return (grad_patches.reshape(images, share, depth), grad_weight)


def solution(mesh):
    placed = (
        P("rows", None, None),
        P("rows", None, None),
        P("rows", None),
        P(None, "protos"),
        P(None, "protos"),
    )
    return jax.shard_map(
        local,
        mesh=mesh,
        in_specs=placed,
        out_specs=(P("rows", "protos", None), P("rows", "protos")),
        check_vma=False,
    )
```

```python
import functools
import math

import jax
import jax.numpy as jnp
from jax import lax
from jax.experimental import pallas as pl
from jax.experimental.pallas import tpu as pltpu
from jax.sharding import PartitionSpec as P

PROTOS = 65536
SK_ITERS = 3
LANES = 128

epsilon = 1e-06
temp_student = 0.1
temp_teacher = 0.07

f32 = jnp.float32
bf16 = jnp.bfloat16


def call(body, outs, ins, scratch=(), limit=8, hbm=0, flops=0, moved=0):
    held = [pltpu.with_memory_space_constraint(array, pltpu.HBM) for array in ins[:hbm]]
    spaces = [pltpu.HBM] * hbm + [pltpu.VMEM] * (len(ins) - hbm)
    return pl.pallas_call(
        body,
        out_shape=[
            (space[0] if space else pltpu.VMEM)(shape, dtype) for shape, dtype, *space in outs
        ],
        in_specs=[pl.BlockSpec(memory_space=space) for space in spaces],
        out_specs=[
            pl.BlockSpec(memory_space=pltpu.HBM if space and space[0] is pltpu.HBM else pltpu.VMEM)
            for _, _, *space in outs
        ],
        scratch_shapes=list(scratch),
        compiler_params=pltpu.CompilerParams(vmem_limit_bytes=limit * 2**20),
        cost_estimate=pl.CostEstimate(flops=flops, bytes_accessed=moved, transcendentals=0),
    )(*held, *ins[hbm:])


def pick(patches_ref, positions, image):
    patches = patches_ref.shape[1]
    masked = positions.shape[0]
    column = lax.broadcasted_iota(jnp.int32, (masked, patches), 1).astype(f32)
    chosen = (column == positions[:, image : image + 1]).astype(bf16)
    return jnp.dot(chosen, patches_ref[image], preferred_element_type=f32)


def lanes_of_rows(parts):
    groups = parts.shape[0] // LANES
    lane = lax.broadcasted_iota(jnp.int32, (LANES, LANES), 1)
    table = jnp.zeros((LANES, LANES), f32)
    for group in range(groups):
        column = jnp.sum(parts[group * LANES : (group + 1) * LANES], axis=1, keepdims=True)
        table = jnp.where(lane == group, column, table)
    table = table.T
    return jnp.concatenate([table[group : group + 1] for group in range(groups)], axis=1)


def fold_lanes(values):
    total = values[:, :LANES]
    for start in range(LANES, values.shape[1], LANES):
        total = total + values[:, start : start + LANES]
    return total


def rows_on_sublanes(line):
    pieces = [
        jnp.broadcast_to(line[:, s : s + LANES], (LANES, LANES)).T
        for s in range(0, line.shape[1], LANES)
    ]
    return jnp.concatenate(pieces, axis=0)


def spread(column, width):
    return jnp.concatenate([column] * (width // LANES), axis=1)


def unit_columns(weight_ref, cols):
    weight = weight_ref[:, cols].astype(f32)
    length = jnp.sqrt(jnp.sum(weight * weight, axis=0, keepdims=True) + epsilon)
    return weight * (1.0 / length), length


TILE = 256
LOG2_E = math.log2(math.e)


def first_body(
    teacher_hbm, teacher_weight_hbm, student_hbm, student_weight_hbm, mask_hbm,
    teacher_exp_ref, cols_ref, student_exp_ref, student_rows_ref, unit_ref, inverse_ref, turned_ref, unit_weight_ref,
    length_ref,
    teacher_ref, teacher_weight_ref, student_ref, student_weight_ref, mask_ref, teacher_bf_ref, student_bf_ref, parts_ref, sems,
):
    images, masked = mask_ref.shape
    protos = teacher_exp_ref.shape[1]
    loads = [
        pltpu.make_async_copy(source, target, sems.at[index])
        for index, (source, target) in enumerate(
            (
                (mask_hbm, mask_ref),
                (teacher_hbm, teacher_ref),
                (teacher_weight_hbm, teacher_weight_ref),
                (student_hbm, student_ref),
                (student_weight_hbm, student_weight_ref),
            )
        )
    ]
    for load in loads[:3]:
        load.start()
    loads[0].wait()
    positions = mask_ref[...].astype(f32).T
    loads[1].wait()
    for load in loads[3:]:
        load.start()
    for image in range(images):
        picked = pick(teacher_ref, positions, image)
        length = jnp.sqrt(jnp.sum(picked * picked, axis=1, keepdims=True) + epsilon)
        rows = slice(image * masked, (image + 1) * masked)
        teacher_bf_ref[rows, :] = (picked * (1.0 / length)).astype(bf16)
    loads[2].wait()

    def teacher_tile(tile, _):
        cols = pl.ds(pl.multiple_of(tile * TILE, TILE), TILE)
        unit = unit_columns(teacher_weight_ref, cols)[0].astype(bf16)
        products = jnp.dot(teacher_bf_ref[...], unit, preferred_element_type=f32)
        exps = jnp.exp2(products * (LOG2_E / temp_teacher))
        teacher_exp_ref[:, cols] = exps
        line = jnp.sum(exps, axis=0, keepdims=True)
        cols_ref[:, :, cols] = jnp.broadcast_to(line[None], (cols_ref.shape[0], 1, TILE))
        return 0

    lax.fori_loop(0, protos // TILE, teacher_tile, 0, unroll=8)
    loads[3].wait()

    for image in range(images):
        picked = pick(student_ref, positions, image)
        inverse = 1.0 / jnp.sqrt(jnp.sum(picked * picked, axis=1, keepdims=True) + epsilon)
        unit = picked * inverse
        rows = slice(image * masked, (image + 1) * masked)
        unit_ref[rows, :] = unit
        student_bf_ref[rows, :] = unit.astype(bf16)
        turned_ref[:, rows] = unit.T.astype(bf16)
        inverse_ref[rows, :] = jnp.broadcast_to(inverse, (masked, LANES))
    parts_ref[...] = jnp.zeros_like(parts_ref)
    loads[4].wait()

    def student_tile(tile, _):
        cols = pl.ds(pl.multiple_of(tile * TILE, TILE), TILE)
        unit, length = unit_columns(student_weight_ref, cols)
        length_ref[:, cols] = length
        unit = unit.astype(bf16)
        unit_weight_ref[:, cols] = unit
        products = jnp.dot(student_bf_ref[...], unit, preferred_element_type=f32)
        exps = jnp.exp2(products * (LOG2_E / temp_student))
        student_exp_ref[:, cols] = exps
        parts_ref[...] += fold_lanes(exps)
        return 0

    lax.fori_loop(0, protos // TILE, student_tile, 0, unroll=8)
    student_rows_ref[...] = lanes_of_rows(parts_ref[...])


def store_copies(out_ref, line):
    out_ref[...] = jnp.broadcast_to(line[None], out_ref.shape)


def columns_body(sums_ref, exp_ref, *refs):
    *rider, scale_ref, rows_ref, parts_ref = refs
    scale = 1.0 / (jnp.sum(sums_ref[...], axis=0) * PROTOS)
    scale_ref[...] = scale
    step = 64

    def block(index, _):
        rows = pl.ds(pl.multiple_of(index * step, step), step)
        total = exp_ref[rows, :LANES] * scale[:, :LANES]
        for start in range(LANES, exp_ref.shape[1], LANES):
            total = total + exp_ref[rows, start : start + LANES] * scale[:, start : start + LANES]
        parts_ref[rows, :] = total
        return 0

    lax.fori_loop(0, exp_ref.shape[0] // step, block, 0, unroll=8)
    line = lanes_of_rows(parts_ref[...])
    peers, _, width = rows_ref.shape
    rows = line.shape[1]
    rows_ref[:, :, :rows] = jnp.broadcast_to(line[None], (peers, 1, rows))
    if rider:
        groups = rider[0].shape[1] // LANES
        for group in range(groups):
            lanes = rider[0][:, group * LANES : (group + 1) * LANES]
            some = slice(group * peers // groups, (group + 1) * peers // groups)
            rows_ref[some, :, rows:] = jnp.broadcast_to(lanes[None], (peers // groups, 1, LANES))


def rows_body(total_rows, sums_ref, exp_ref, cols_ref, *refs):
    *rider, scale_ref, parts_ref = refs
    sums = jnp.sum(sums_ref[...], axis=0)
    line = 1.0 / (sums[:, : exp_ref.shape[0]] * total_rows)
    if rider:
        rider[0][...] = sums[:, exp_ref.shape[0] :]
    scale_ref[...] = rows_on_sublanes(line)
    width = exp_ref.shape[1]
    parts_ref[...] = jnp.zeros_like(parts_ref)
    step = 64

    def block(index, _):
        rows = pl.ds(pl.multiple_of(index * step, step), step)
        scale = scale_ref[rows, :]
        for start in range(0, width, LANES):
            product = exp_ref[rows, start : start + LANES] * scale
            total = product[0:8]
            for r in range(8, step, 8):
                total = total + product[r : r + 8]
            parts_ref[:, start : start + LANES] += total
        return 0

    lax.fori_loop(0, exp_ref.shape[0] // step, block, 0, unroll=8)
    store_copies(cols_ref, jnp.sum(parts_ref[...], axis=0, keepdims=True))


def feature_body(
    total_rows,
    sums_ref, student_ref, cols_ref, teacher_exp_ref, student_exp_ref, unit_weight_ref, unit_ref, inverse_ref,
    mask_ref,
    placed_hbm, score_hbm, row_ref, total_ref, sum_ref, score_ref, placed_ref, sems,
):
    rows = teacher_exp_ref.shape[0]
    row_ref[...] = rows_on_sublanes(1.0 / (jnp.sum(sums_ref[...], axis=0) * total_rows))
    groups = rows // LANES
    step = student_ref.shape[0] // groups
    totals = jnp.concatenate([student_ref[group * step][:, rows:] for group in range(groups)], axis=1)
    total_ref[...] = rows_on_sublanes((1.0 / temp_student) / totals)

    protos = teacher_exp_ref.shape[1]
    halves = [slice(0, protos // 2), slice(protos // 2, protos)]
    stores = [
        pltpu.make_async_copy(score_ref.at[:, half], score_hbm.at[:, half], sems.at[index])
        for index, half in enumerate(halves)
    ]

    def score_of(half):
        for start in range(half.start, half.stop, TILE):
            cols = slice(start, start + TILE)
            target = teacher_exp_ref[:, cols] * spread(row_ref[...], TILE)
            target = target * (cols_ref[:, cols] * (total_rows / temp_student))
            score = (student_exp_ref[:, cols] * spread(total_ref[...], TILE) - target).astype(bf16)
            score_ref[:, cols] = score

    def product(half):
        return lax.dot_general(
            score_ref[:, half], unit_weight_ref[:, half], (((1,), (1,)), ((), ())), preferred_element_type=f32
        )

    score_of(halves[0])
    stores[0].start()
    sum_ref[...] = product(halves[0])
    score_of(halves[1])
    stores[1].start()
    sum_ref[...] += product(halves[1])
    images, masked = mask_ref.shape
    width = unit_ref.shape[1]
    shares = placed_ref.shape[0]
    share = placed_ref.shape[1] // images
    patch = lax.broadcasted_iota(jnp.int32, (shares * share, 2 * masked), 0)

    placed_stores = []
    for image in range(images):
        rows = slice(image * masked, (image + 1) * masked)
        unit = unit_ref[rows, :]
        total = sum_ref[rows, :]
        projection = jnp.sum(unit * total, axis=1, keepdims=True)
        gradient = (total - unit * projection) * spread(inverse_ref[rows, :], width)
        high = gradient.astype(bf16)
        low = (gradient - high.astype(f32)).astype(bf16)
        positions = mask_ref[image : image + 1, :]
        chosen = (patch == jnp.concatenate([positions, positions], axis=1)).astype(bf16)
        placed = jnp.dot(chosen, jnp.concatenate([high, low], axis=0), preferred_element_type=f32)
        where = pl.ds(image * share, share)
        placed_ref[:, where, :] = placed.reshape(shares, share, width)
        placed_stores.append(
            pltpu.make_async_copy(placed_ref.at[:, where], placed_hbm.at[:, where], sems.at[2 + image])
        )
        placed_stores[-1].start()
    for store in stores + placed_stores:
        store.wait()


def weight_body(
    score_hbm, weight_hbm, turned_ref, length_ref, mine_ref, other_ref, score_ref, weight_ref, sems
):
    levels, share = mine_ref.shape[:2]
    me = lax.axis_index("rows")
    core, level = me % 2, me // 2
    protos = weight_ref.shape[1]
    half = protos // 2
    weight_load = pltpu.make_async_copy(weight_hbm, weight_ref, sems.at[2])
    loads = [
        pltpu.make_async_copy(
            score_hbm.at[:, pl.ds(start, half)], score_ref.at[:, pl.ds(start, half)], sems.at[index]
        )
        for index, start in enumerate((0, half))
    ]
    for load in (loads[0], weight_load, loads[1]):
        load.start()
    weight_load.wait()
    for start in range(0, protos, TILE):
        cols = slice(start, start + TILE)
        if start % half == 0:
            loads[start // half].wait()
        total = jnp.dot(turned_ref[...], score_ref[:, cols], preferred_element_type=f32)
        inverse = 1.0 / length_ref[:, cols]
        unit = weight_ref[:, cols].astype(f32) * inverse
        dots = jnp.sum(unit * total, axis=0, keepdims=True)
        gradient = ((total - unit * dots) * inverse).reshape(levels, 2, share, TILE)
        for z in range(levels):
            place = pl.ds((z + levels - level) % levels, 1)
            mine_ref[place, :, cols] = jnp.where(core == 0, gradient[z, 0], gradient[z, 1])[None]
            other_ref[place, :, cols] = jnp.where(core == 0, gradient[z, 1], gradient[z, 0])[None]


def total_body(parts_ref, out_ref):
    out_ref[...] = jnp.sum(parts_ref[...], axis=0)


def everyones(copies, axis):
    return lax.all_to_all(copies, axis, 0, 0, tiled=True)


def send_rows(values, to):
    return lax.ppermute(values, "rows", [(i, to(i)) for i in range(lax.axis_size("rows"))])


def ring_share(parts, levels):
    def along(values, by):
        return send_rows(values, lambda i: (i + 2 * by) % (2 * levels))

    last = levels // 2
    total = parts[0]
    if levels > 1:
        up = parts[last]
        for k in range(last - 1, 0, -1):
            up = along(up, 1) + parts[k]
        total = total + along(up, 1)
    if levels > 2:
        down = parts[last + 1]
        for k in range(last + 2, levels):
            down = along(down, -1) + parts[k]
        total = total + along(down, -1)
    return total


def local(student_patches, teacher_patches, mask_index, student_weight, teacher_weight):
    images, patches, depth = student_patches.shape
    masked = mask_index.shape[1]
    rows = images * masked
    row_devices = lax.axis_size("rows")
    proto_devices = lax.axis_size("protos")
    total_rows = float(rows * row_devices)
    protos = student_weight.shape[1]
    work = 2 * rows * protos * depth

    teacher_exp, column_part, student_exp, student_part, unit, inverse, turned, unit_weight, length = call(
        first_body,
        [
            ((rows, protos), f32),
            ((row_devices, 1, protos), f32),
            ((rows, protos), f32),
            ((1, rows), f32),
            ((rows, depth), f32),
            ((rows, LANES), f32),
            ((depth, rows), bf16),
            ((depth, protos), bf16),
            ((1, protos), f32),
        ],
        (teacher_patches, teacher_weight, student_patches, student_weight, mask_index),
        [
            pltpu.VMEM(teacher_patches.shape, bf16),
            pltpu.VMEM(teacher_weight.shape, bf16),
            pltpu.VMEM(student_patches.shape, bf16),
            pltpu.VMEM(student_weight.shape, bf16),
            pltpu.VMEM(mask_index.shape, jnp.int32),
            pltpu.VMEM((rows, depth), bf16),
            pltpu.VMEM((rows, depth), bf16),
            pltpu.VMEM((rows, LANES), f32),
            pltpu.SemaphoreType.DMA((5,)),
        ],
        limit=12, hbm=5, flops=2 * work, moved=2**23,
    )
    rider = student_part
    for sweep in range(SK_ITERS):
        column_sums = everyones(column_part, "rows")
        riders = [rider] if sweep < 2 else []
        col_scale, row_part = call(
            columns_body,
            [((1, protos), f32), ((proto_devices, 1, rows + LANES * len(riders)), f32)],
            (column_sums, teacher_exp, *riders),
            [pltpu.VMEM((rows, LANES), f32)],
            flops=2 * rows * protos, moved=2**23,
        )
        row_sums = everyones(row_part, "protos")
        if sweep == 1:
            student_sums = row_sums
        if sweep < SK_ITERS - 1:
            column_part, *riding = call(
                functools.partial(rows_body, total_rows),
                [((row_devices, 1, protos), f32)] + [((1, LANES), f32)] * (sweep == 0),
                (row_sums, teacher_exp),
                [pltpu.VMEM((rows, LANES), f32), pltpu.VMEM((8, protos), f32)],
                flops=2 * rows * protos, moved=2**23,
            )
            if sweep == 0:
                (rider,) = riding
    share = patches // proto_devices
    levels = row_devices // 2
    placed, score = call(
        functools.partial(feature_body, total_rows),
        [((proto_devices, images * share, depth), f32, pltpu.HBM), ((rows, protos), bf16, pltpu.HBM)],
        (row_sums, student_sums, col_scale, teacher_exp, student_exp, unit_weight, unit, inverse, mask_index),
        [
            pltpu.VMEM((rows, LANES), f32),
            pltpu.VMEM((rows, LANES), f32),
            pltpu.VMEM((rows, depth), f32),
            pltpu.VMEM((rows, protos), bf16),
            pltpu.VMEM((proto_devices, images * share, depth), f32),
            pltpu.SemaphoreType.DMA((2 + images,)),
        ],
        limit=16, flops=work, moved=2**24,
    )
    arrived = everyones(placed, "protos")
    mine, other = call(
        weight_body,
        [((levels, depth // row_devices, protos), f32)] * 2,
        (score, student_weight, turned, length),
        [
            pltpu.VMEM((rows, protos), bf16),
            pltpu.VMEM(student_weight.shape, bf16),
            pltpu.SemaphoreType.DMA((3,)),
        ],
        limit=12, hbm=2,
    )
    grad_weight = ring_share(mine + send_rows(other, lambda i: i ^ 1), levels)
    (grad_patches,) = call(
        total_body,
        [(arrived.shape[1:], f32, jax.ShapeDtypeStruct)],
        (arrived,),
    )
    return (grad_patches.reshape(images, share, depth), grad_weight)


def solution(mesh):
    placed = (
        P("rows", None, None),
        P("rows", None, None),
        P("rows", None),
        P(None, "protos"),
        P(None, "protos"),
    )
    return jax.shard_map(
        local,
        mesh=mesh,
        in_specs=placed,
        out_specs=(P("rows", "protos", None), P("rows", "protos")),
        check_vma=False,
    )
```
